32 devices in a mesh: dp: 16 (over z, y, core), shard: 2 (over x).
Axes of the slice: x: 2, y: 2, z: 4, core: 2. Of those that a mesh axis runs over, the one named last changes fastest.
Arguments:
- tokens: bfloat16 [32, 512, 1024], P('dp', 'shard'), may hold values from -6 to 6
- cotangent: bfloat16 [32, 512, 1024], P('dp', 'shard'), may hold values from -6 to 6
- lengths: int32 [32], P('dp'), may hold values from 1 to 512, as said below
- entry_weight: float32 [1024, 4096], P(('dp', 'shard')), may hold values from -0.1875 to 0.1875
- output_weight: float32 [2048, 1024], P(('dp', 'shard')), may hold values from -0.5 to 0.5
- gate_weight: float32 [1024, 6144], P(('dp', 'shard')), may hold values from -0.1875 to 0.1875
- down_weight: float32 [3072, 1024], P(('dp', 'shard')), may hold values from -0.21875 to 0.21875
- entry_first: float32 [1024, 4096], P(('dp', 'shard')), may hold values from -80 to 80
- output_first: float32 [2048, 1024], P(('dp', 'shard')), may hold values from -16 to 16
- gate_first: float32 [1024, 6144], P(('dp', 'shard')), may hold values from -48 to 48
- down_first: float32 [3072, 1024], P(('dp', 'shard')), may hold values from -48 to 48
- entry_second: float32 [1024, 4096], P(('dp', 'shard')), may hold values from 655.36 to 2621.44
- output_second: float32 [2048, 1024], P(('dp', 'shard')), may hold values from 26.2144 to 104.8576
- gate_second: float32 [1024, 6144], P(('dp', 'shard')), may hold values from 278.528 to 1114.112
- down_second: float32 [3072, 1024], P(('dp', 'shard')), may hold values from 235.9296 to 943.7184
- gains: float32 [2304], replicated, may hold values from 0.5 to 1.5
- gains_first: float32 [2304], replicated, may hold values from -224 to 224
- gains_second: float32 [2304], replicated, may hold values from 5242.88 to 20971.52
Outputs:
- block_out: bfloat16 [32, 512, 1024], P('dp', 'shard')
- token_grad: float32 [32, 512, 1024], P('dp', 'shard')
- new_entry: float32 [1024, 4096], P(('dp', 'shard'))
- new_entry_first: float32 [1024, 4096], P(('dp', 'shard'))
- new_entry_second: float32 [1024, 4096], P(('dp', 'shard'))
- new_output: float32 [2048, 1024], P(('dp', 'shard'))
- new_output_first: float32 [2048, 1024], P(('dp', 'shard'))
- new_output_second: float32 [2048, 1024], P(('dp', 'shard'))
- new_gate: float32 [1024, 6144], P(('dp', 'shard'))
- new_gate_first: float32 [1024, 6144], P(('dp', 'shard'))
- new_gate_second: float32 [1024, 6144], P(('dp', 'shard'))
- new_down: float32 [3072, 1024], P(('dp', 'shard'))
- new_down_first: float32 [3072, 1024], P(('dp', 'shard'))
- new_down_second: float32 [3072, 1024], P(('dp', 'shard'))
- new_gains: float32 [2304], replicated
- new_gains_first: float32 [2304], replicated
- new_gains_second: float32 [2304], replicated
The draws below stay inside these ranges and needn't reach their ends.
Inputs may be any that keep to these rules, and one draw needn't show every extreme that they name: `lengths`: in each aligned block of 2 sequences (the sequences of one data group) one has length exactly 512.
All inputs are finite; a program needn't handle non-finite values.
Results may differ from the reference program's by a relative error of at most 0.012.
The reference program's roundings to bfloat16 on the way count: a program that leaves them out, or rounds other values in their place, can miss the bound.
Values may be sent and summed in bfloat16 or wider, within the bound.
No kernel may reach another device: no remote copies, remote signals or barrier semaphores. Data moves between devices by JAX's collectives and lax.ppermute only.
A program may use at most 320 MiB of HBM per device.

```python
import math
import jax
import jax.numpy as jnp
from jax import lax

D = 1024
HEADS = 16
KV_HEADS = 8
HEAD_DIM = 128
FF = 3072
SEQ_LEN = 512
SEQ_GROUP = 2
STEP = 10
SEQS = 32
SLOTS = 16384
QKV = 4096
GAINS = 2304


def draw_lengths(key, part):
    key = jax.random.fold_in(key, 11)
    key_spans, key_chosen = jax.random.split(key)
    drawn = jax.random.randint(key_spans, (SEQS,), 1, SEQ_LEN + 1)
    chosen = jax.random.randint(key_chosen, (SEQS // SEQ_GROUP,), 0, SEQ_GROUP)
    longest = jnp.arange(SEQS) % SEQ_GROUP == jnp.repeat(chosen, SEQ_GROUP)
    return jnp.where(longest, SEQ_LEN, drawn).astype(jnp.int32)


def steps_of(rng, extent, cuts, smallest, largest):
    level = 1.0
    for position, shards_of in cuts:
        draws = jax.random.uniform(jax.random.fold_in(jax.random.fold_in(rng, 6), position), (shards_of,), jnp.float32, smallest / len(cuts), largest / len(cuts))
        level = level * jnp.repeat(jnp.exp(draws), extent[position] // shards_of).reshape((-1,) + (1,) * (len(extent) - 1 - position))
    return level


def gaussian(stream_key, shape, spread, reach, cuts=(), dtype=jnp.bfloat16):
    entries = jax.random.normal(stream_key, shape, jnp.float32) * spread
    if len(cuts) > 0:
        entries = steps_of(stream_key, shape, cuts, -0.22, 0.18) * entries
    return jnp.clip(entries, min=-reach, max=reach).astype(dtype)


def setup_inputs(seed: int = 0) -> dict:
    key_list = jax.random.split(jax.random.key(seed), 19)
    tokens = gaussian(key_list[0], (SEQS, SEQ_LEN, D), 1.0, 6.0, ((0, 16), (1, 2)))
    cotangent = gaussian(key_list[1], (SEQS, SEQ_LEN, D), 1.0, 6.0, ((0, 16), (1, 2)))
    lengths = draw_lengths(jax.random.fold_in(key_list[18], 71), 0)
    entry_weight = gaussian(key_list[3], (D, QKV), D ** -0.5, 0.1875, ((0, 32),), jnp.float32)
    output_weight = gaussian(key_list[4], (HEADS * HEAD_DIM, D), (HEADS * HEAD_DIM // 16) ** -0.5, 0.5, ((0, 32),), jnp.float32)
    gate_weight = gaussian(key_list[5], (D, 2 * FF), D ** -0.5, 0.1875, ((0, 32),), jnp.float32)
    down_weight = gaussian(key_list[6], (FF, D), (FF // 4) ** -0.5, 0.21875, ((0, 32),), jnp.float32)
    entry_first = gaussian(key_list[7], (D, QKV), (0.1 * SLOTS ** 0.5), 80.0, ((0, 32),), jnp.float32)
    output_first = gaussian(key_list[8], (HEADS * HEAD_DIM, D), (0.02 * SLOTS ** 0.5), 16.0, ((0, 32),), jnp.float32)
    gate_first = gaussian(key_list[9], (D, 2 * FF), (0.065 * SLOTS ** 0.5), 48.0, ((0, 32),), jnp.float32)
    down_first = gaussian(key_list[10], (FF, D), (0.06 * SLOTS ** 0.5), 48.0, ((0, 32),), jnp.float32)
    entry_second = jnp.clip(jnp.exp(math.log(2621.44) - 1.3862944 * jax.random.uniform(key_list[11], (D, QKV), jnp.float32) ** steps_of(key_list[11], (D, QKV), ((0, 32),), -0.2, 0.2)), 655.36, 2621.44)
    output_second = jnp.clip(jnp.exp(math.log(104.8576) - 1.3862944 * jax.random.uniform(key_list[12], (HEADS * HEAD_DIM, D), jnp.float32) ** steps_of(key_list[12], (HEADS * HEAD_DIM, D), ((0, 32),), -0.2, 0.2)), 26.2144, 104.8576)
    gate_second = jnp.clip(jnp.exp(math.log(1114.112) - 1.3862944 * jax.random.uniform(key_list[13], (D, 2 * FF), jnp.float32) ** steps_of(key_list[13], (D, 2 * FF), ((0, 32),), -0.2, 0.2)), 278.528, 1114.112)
    down_second = jnp.clip(jnp.exp(math.log(943.7184) - 1.3862944 * jax.random.uniform(key_list[14], (FF, D), jnp.float32) ** steps_of(key_list[14], (FF, D), ((0, 32),), -0.2, 0.2)), 235.9296, 943.7184)
    gains = jnp.clip(1.0 + 0.1 * jax.random.normal(key_list[15], (GAINS,), jnp.float32), 0.5, 1.5)
    gains_first = gaussian(key_list[16], (GAINS,), (0.28 * SLOTS ** 0.5), 224.0, (), jnp.float32)
    gains_second = jnp.clip(jnp.exp(jax.random.uniform(key_list[17], (GAINS,), jnp.float32, math.log(5242.88), math.log(20971.52))), 5242.88, 20971.52)
    return dict(tokens=tokens, cotangent=cotangent, lengths=lengths, entry_weight=entry_weight, output_weight=output_weight, gate_weight=gate_weight, down_weight=down_weight, entry_first=entry_first, output_first=output_first, gate_first=gate_first, down_first=down_first, entry_second=entry_second, output_second=output_second, gate_second=gate_second, down_second=down_second, gains=gains, gains_first=gains_first, gains_second=gains_second)


EPS = 1e-06
THETA = 1000000.0
NEG = -1e+30
BETA_ONE = 0.9
BETA_TWO = 0.95
ADAM_EPS = 1e-08
DECAY = 0.1
RATE_MATRIX = 0.03
RATE_OUTPUT = 0.06
RATE_GAIN = 0.25
HIGH = lax.Precision.HIGHEST

@jax.custom_vjp
def low(v):
    return lax.optimization_barrier(v.astype(jnp.bfloat16)).astype(jnp.float32)

@jax.custom_vjp
def low_back(v):
    return v

def low_keep(v):
    return (low(v), None)

def low_pass(kept, grad):
    return (grad,)

def back_keep(v):
    return (v, None)

def back_low(kept, grad):
    return (low(grad),)
low.defvjp(low_keep, low_pass)
low_back.defvjp(back_keep, back_low)

def norm_rows(values, gain):
    return values * lax.rsqrt(lax.optimization_barrier(jnp.mean(values * values, axis=-1, keepdims=True)) + EPS) * gain

def rotate(values, cosine, sine):
    half = values.shape[-1] // 2
    leading = values[..., :half]
    trailing = values[..., half:]
    return jnp.concatenate([leading * cosine - trailing * sine, trailing * cosine + leading * sine], axis=-1)

def angles(positions):
    freqs = THETA ** (-(jnp.arange(HEAD_DIM // 2).astype(jnp.float32) * 2.0) / HEAD_DIM)
    turned = positions.astype(jnp.float32)[:, None] * freqs[None, :]
    return (jnp.cos(turned), jnp.sin(turned))

def forward(inputs, entry, output, gate, down, gain_vec, live, cosine, sine):
    seq_count = inputs.shape[0]
    span_len = inputs.shape[1]
    group_size = HEADS // KV_HEADS
    query_cols = HEADS * HEAD_DIM
    key_cols = KV_HEADS * HEAD_DIM
    g_attn = gain_vec[:D]
    g_mlp = gain_vec[D:2 * D]
    g_query = gain_vec[2 * D:2 * D + HEAD_DIM]
    g_key = gain_vec[2 * D + HEAD_DIM:]
    normed = low(norm_rows(inputs, g_attn))
    projected = jnp.einsum('bld,dc->blc', normed, low(entry), precision=HIGH)
    query = low_back(projected[..., :query_cols]).reshape(seq_count, span_len, HEADS, HEAD_DIM)
    key_raw = low_back(projected[..., query_cols:query_cols + key_cols]).reshape(seq_count, span_len, KV_HEADS, HEAD_DIM)
    value = low(low_back(projected[..., query_cols + key_cols:])).reshape(seq_count, span_len, KV_HEADS, HEAD_DIM)
    cos_four = cosine[None, :, None, :]
    sin_four = sine[None, :, None, :]
    query_rot = low(rotate(norm_rows(query, g_query), cos_four, sin_four))
    query_rot = query_rot.reshape(seq_count, span_len, KV_HEADS, group_size, HEAD_DIM)
    key_rot = low(rotate(norm_rows(key_raw, g_key), cos_four, sin_four))
    raw = jnp.einsum('bqgrd,bkgd->bgrqk', query_rot, key_rot, precision=HIGH) * HEAD_DIM ** (-0.5)
    place = jnp.arange(span_len)
    allowed = (place[None, None, :] <= place[None, :, None]) & live[:, None, :]
    scores = jnp.where(allowed[:, None, None], low_back(raw), NEG)
    probs = jax.nn.softmax(scores, axis=-1)
    context = jnp.einsum('bgrqk,bkgd->bqgrd', low(probs), value, precision=HIGH)
    context = low_back(low(context)).reshape(seq_count, span_len, query_cols)
    attended = low_back(jnp.einsum('blh,hd->bld', context, low(output), precision=HIGH))
    middle = inputs + attended
    normed_two = low(norm_rows(middle, g_mlp))
    both = jnp.einsum('bld,dc->blc', normed_two, low(gate), precision=HIGH)
    gate_val = low_back(both[..., :FF])
    up_val = low_back(both[..., FF:])
    hidden = low(jax.nn.silu(gate_val) * up_val)
    result = middle + jnp.einsum('blf,fd->bld', hidden, low(down), precision=HIGH)
    return result * live[..., None].astype(jnp.float32)

def adam(weight, moment_one, moment_two, grad, rate, decay):
    new_one = BETA_ONE * moment_one + (1.0 - BETA_ONE) * grad
    new_two = BETA_TWO * moment_two + (1.0 - BETA_TWO) * grad * grad
    ratio = new_one / (1.0 - BETA_ONE ** STEP) / (jnp.sqrt(new_two / (1.0 - BETA_TWO ** STEP)) + ADAM_EPS)
    return (weight - rate * (ratio + decay * weight), new_one, new_two)

def reference(tokens, cotangent, lengths, entry_weight, output_weight, gate_weight, down_weight, entry_first, output_first, gate_first, down_first, entry_second, output_second, gate_second, down_second, gains, gains_first, gains_second):
    group_count = math.gcd(SEQS, max(1, 4096 // SEQ_LEN))
    rounds = SEQS // group_count
    place = jnp.arange(SEQ_LEN)
    cosine, sine = angles(place)
    live_all = place[None, :] < lengths[:, None]
    inputs_all = tokens.astype(jnp.float32).reshape(rounds, group_count, SEQ_LEN, D)
    backs_all = cotangent.astype(jnp.float32).reshape(rounds, group_count, SEQ_LEN, D)
    lives = live_all.reshape(rounds, group_count, SEQ_LEN)
    weights = (entry_weight, output_weight, gate_weight, down_weight, gains)

    def one_round(carry, pieces):
        inputs, backs, live = pieces

        def apply(inputs, entry, output, gate, down, gain_vec):
            return forward(inputs, entry, output, gate, down, gain_vec, live, cosine, sine)
        result, pull = jax.vjp(apply, inputs, *weights)
        grads = pull(backs)
        totals = tuple((total + grad for total, grad in zip(carry, grads[1:])))
        return (totals, (result.astype(jnp.bfloat16), grads[0]))
    start = tuple((jnp.zeros_like(weight) for weight in weights))
    totals, (results, input_grads) = lax.scan(one_round, start, (inputs_all, backs_all, lives))
    block_out = results.reshape(SEQS, SEQ_LEN, D)
    token_grad = input_grads.reshape(SEQS, SEQ_LEN, D)
    new_entry, new_entry_first, new_entry_second = adam(entry_weight, entry_first, entry_second, totals[0], RATE_MATRIX, DECAY)
    new_output, new_output_first, new_output_second = adam(output_weight, output_first, output_second, totals[1], RATE_OUTPUT, DECAY)
    new_gate, new_gate_first, new_gate_second = adam(gate_weight, gate_first, gate_second, totals[2], RATE_MATRIX, DECAY)
    new_down, new_down_first, new_down_second = adam(down_weight, down_first, down_second, totals[3], RATE_MATRIX, DECAY)
    new_gains, new_gains_first, new_gains_second = adam(gains, gains_first, gains_second, totals[4], RATE_GAIN, 0.0)
    return (block_out, token_grad, new_entry, new_entry_first, new_entry_second, new_output, new_output_first, new_output_second, new_gate, new_gate_first, new_gate_second, new_down, new_down_first, new_down_second, new_gains, new_gains_first, new_gains_second)
```

```python
import jax
import jax.numpy as jnp
from jax import lax
from jax.experimental import pallas as pl
from jax.experimental.pallas import tpu as pltpu
from jax.sharding import PartitionSpec as P

D = 1024
HEADS = 16
KV_HEADS = 8
HEAD_DIM = 128
FF = 3072
STEP = 10


EPS = 1e-06
THETA = 1000000.0
NEG = -1e30
BETA_ONE = 0.9
BETA_TWO = 0.95
ADAM_EPS = 1e-08
DECAY = 0.1
RATE_MATRIX = 0.03
RATE_OUTPUT = 0.06
RATE_GAIN = 0.25


def norm_rows(values, gain):
    factor = lax.rsqrt(jnp.mean(values * values, axis=-1, keepdims=True) + EPS)
    return (values * factor * gain, factor)


def norm_back(values, factor, gain, incoming):
    normal = values * factor
    scaled = incoming * gain
    inner = jnp.mean(scaled * normal, axis=-1, keepdims=True)
    return (factor * (scaled - normal * inner), incoming * normal)


def rotate(values, cosine, sine, direction):
    half = values.shape[-1] // 2
    leading = values[..., :half]
    trailing = values[..., half:]
    return jnp.concatenate(
        [
            leading * cosine - direction * trailing * sine,
            trailing * cosine + direction * leading * sine,
        ],
        axis=-1,
    )


def angles(positions):
    freqs = THETA ** (-(jnp.arange(HEAD_DIM // 2).astype(jnp.float32) * 2.0) / HEAD_DIM)
    turned = positions.astype(jnp.float32)[:, None] * freqs[None, :]
    return (jnp.cos(turned), jnp.sin(turned))


def adam(weight, moment_one, moment_two, grad, rate, decay):
    new_one = BETA_ONE * moment_one + (1.0 - BETA_ONE) * grad
    new_two = BETA_TWO * moment_two + (1.0 - BETA_TWO) * grad * grad
    ratio = (
        new_one / (1.0 - BETA_ONE**STEP) / (jnp.sqrt(new_two / (1.0 - BETA_TWO**STEP)) + ADAM_EPS)
    )
    return (weight - rate * (ratio + decay * weight), new_one, new_two)


def reduce_pair(grad_left, grad_right):
    replicas = lax.axis_size("dp")
    members = lax.axis_size("shard")
    owners = replicas * members
    left_cols = grad_left.shape[1]
    right_cols = grad_right.shape[1]
    left_rows = grad_left.shape[0] // owners
    right_rows = grad_right.shape[0] // owners
    left_owned, right_owned = (
        lax.psum_scatter(grad_left.reshape(-1), ("dp", "shard"), scatter_dimension=0, tiled=True),
        lax.psum_scatter(grad_right.reshape(-1), ("dp", "shard"), scatter_dimension=0, tiled=True),
    )
    return (left_owned.reshape(left_rows, left_cols), right_owned.reshape(right_rows, right_cols))


class Grid:
    def __init__(self, replicas):
        self.deep = replicas // 4
        index = lax.axis_index("dp")
        self.z = index // 4
        self.y = (index // 2) % 2
        self.c = index % 2
        self.x = lax.axis_index("shard")

    def pairs(self, turn):
        places = [
            (z, y, c, x)
            for z in range(self.deep)
            for y in range(2)
            for c in range(2)
            for x in range(2)
        ]
        flat = lambda z, y, c, x: ((z * 2 + y) * 2 + c) * 2 + x
        return [(flat(*p), flat(*turn(*p))) for p in places]

    def send(self, values, turn):
        return lax.ppermute(values, ("dp", "shard"), self.pairs(turn))

    def over_x(self, values):
        return self.send(values, lambda z, y, c, x: (z, y, c, 1 - x))

    def over_y(self, values):
        return self.send(values, lambda z, y, c, x: (z, 1 - y, c, x))

    def over_core(self, values):
        return self.send(values, lambda z, y, c, x: (z, y, 1 - c, x))

    def along_z(self, values, step):
        return self.send(values, lambda z, y, c, x: ((z + step) % self.deep, y, c, x))

    def up_x(self, values):
        flat = [p for p in self.pairs(lambda z, y, c, x: (z, y, c, 1 - x)) if p[0] % 2 == 0]
        return lax.ppermute(values, ("dp", "shard"), flat)

    def down_x(self, values):
        flat = [p for p in self.pairs(lambda z, y, c, x: (z, y, c, 1 - x)) if p[0] % 2 == 1]
        return lax.ppermute(values, ("dp", "shard"), flat)


def pick(values, index, axis):
    return lax.dynamic_index_in_dim(values, index, axis, keepdims=False)


def place_blocks(grid, own, sibling, rows, cols):
    deep = grid.deep
    half = deep // 2
    places = jnp.stack([grid.z, grid.y, grid.c, grid.x]).astype(jnp.int32)
    spans = [(0, deep, 0, 0), (0, deep, 0, 1), (0, deep, 1, 0), (0, half, 1, 1), (half, deep, 1, 1)]

    def kernel(place_ref, *refs):
        ins, out, held, sems, sent = refs[:10], refs[10], refs[11], refs[12], refs[13]
        z, y, c, x = [place_ref[i] for i in range(4)]
        copies = []
        for core in range(2):
            for piece, (first, last, dy, dx) in enumerate(spans):
                for step in range(first, last):
                    zz = lax.rem(z - step + deep, deep)
                    yy = lax.rem(y + dy, 2)
                    cc = lax.rem(c + core, 2)
                    xx = lax.rem(x + dx, 2)
                    block = ((zz * 2 + yy) * 2 + cc) * 2 + xx
                    turn = len(copies)
                    copies.append(
                        (
                            pltpu.make_async_copy(
                                ins[core * 5 + piece].at[step - first],
                                held.at[turn],
                                sems.at[turn],
                            ),
                            pltpu.make_async_copy(held.at[turn], out.at[block], sent.at[turn]),
                        )
                    )
        for arrive, leave in copies:
            arrive.start()
        for arrive, leave in copies:
            arrive.wait()
            leave.start()
        for arrive, leave in copies:
            leave.wait()

    blocks = deep * 8
    whole = pl.pallas_call(
        kernel,
        out_shape=jax.ShapeDtypeStruct((blocks, rows, cols), jnp.bfloat16),
        in_specs=[pl.BlockSpec(memory_space=pltpu.SMEM)] + [pl.BlockSpec(memory_space=pl.ANY)] * 10,
        out_specs=pl.BlockSpec(memory_space=pl.ANY),
        scratch_shapes=[
            pltpu.VMEM((blocks, rows, cols), jnp.bfloat16),
            pltpu.SemaphoreType.DMA((blocks,)),
            pltpu.SemaphoreType.DMA((blocks,)),
        ],
        compiler_params=pltpu.CompilerParams(vmem_limit_bytes=blocks * rows * cols * 2 + 2**21),
        cost_estimate=pl.CostEstimate(
            flops=0, bytes_accessed=blocks * rows * cols * 4, transcendentals=0
        ),
        name="place_blocks",
    )(places, *own, *sibling)
    return whole.reshape(blocks * rows, cols)


def gather_rows(grid, shard, after_column=()):
    deep = grid.deep
    half = deep // 2
    rows, cols = shard.shape
    column = jnp.stack([shard] + [grid.along_z(shard, step) for step in range(1, deep)])
    ready = tie(column, *after_column)
    x_column = grid.over_x(ready)
    y_column = grid.over_y(ready)
    first = grid.over_y(x_column[:half])
    second = grid.over_x(y_column[half:])
    own = (ready, x_column, y_column, first, second)
    sibling = tuple(grid.over_core(piece) for piece in own)
    return place_blocks(grid, own, sibling, rows, cols), (column, first, second)


def halves(grid, values):
    cols = values.shape[1] // 2
    kept = lax.dynamic_slice_in_dim(values, grid.c * cols, cols, 1)
    sent = lax.dynamic_slice_in_dim(values, (1 - grid.c) * cols, cols, 1)
    return kept, sent


def both_cores(grid, left, kept, sent):
    left_all = jnp.concatenate([left, grid.over_core(left)])
    right_all = jnp.concatenate([kept, grid.over_core(sent)])
    return lax.dot_general(
        left_all, right_all, (((0,), (0,)), ((), ())), preferred_element_type=jnp.float32
    ).astype(jnp.bfloat16)


def added(kept, arrived):
    return (kept.astype(jnp.float32) + arrived.astype(jnp.float32)).astype(jnp.bfloat16)


def tie(value, *after):
    if not after:
        return value

    def kernel(*refs):
        pass

    return pl.pallas_call(
        kernel,
        out_shape=jax.ShapeDtypeStruct(value.shape, value.dtype),
        in_specs=[pl.BlockSpec(memory_space=pl.ANY)] * (1 + len(after)),
        out_specs=pl.BlockSpec(memory_space=pl.ANY),
        input_output_aliases={0: 0},
        cost_estimate=pl.CostEstimate(flops=0, bytes_accessed=0, transcendentals=0),
        name="tie",
    )(value, *after)


def scatter_one(grid, partial, *after):
    rows = partial.shape[0] // (grid.deep * 8)
    blocks = partial.reshape(grid.deep, 2, 2, 2, rows, partial.shape[1])
    first, second = blocks[:, :, 0], blocks[:, :, 1]
    first_sent = tie(pick(first, 1 - grid.y, 1), *after)
    second_sent = tie(pick(second, 1 - grid.x, 2), *after)
    return (
        added(pick(first, grid.y, 1), grid.over_y(first_sent)),
        added(pick(second, grid.x, 2), grid.over_x(second_sent)),
    ), (first_sent, second_sent)


def scatter_two(grid, sums, *after):
    first, second = sums
    first_sent = tie(pick(first, 1 - grid.x, 1), *after)
    second_sent = tie(pick(second, 1 - grid.y, 1), *after)
    return jnp.stack(
        [
            added(pick(first, grid.x, 1), grid.over_x(first_sent)),
            added(pick(second, grid.y, 1), grid.over_y(second_sent)),
        ],
        axis=1,
    )


def scatter_three(grid, chip):
    total = pick(chip, grid.z, 0).astype(jnp.float32)
    for step in range(1, grid.deep):
        sent = pick(chip, (grid.z + step) % grid.deep, 0)
        total = total + grid.along_z(sent, step).astype(jnp.float32)
    kept = pick(total, grid.c, 0)
    arrived = grid.over_core(pick(total, 1 - grid.c, 0))
    return jnp.where(
        grid.c == 0,
        jnp.concatenate([kept, arrived], axis=1),
        jnp.concatenate([arrived, kept], axis=1),
    )


def sum_all(grid, values):
    values = values + grid.over_core(values)
    values = values + grid.over_x(values)
    values = values + grid.over_y(values)
    step = 1
    while step < grid.deep:
        values = values + grid.send(values, lambda z, y, c, x: (z ^ step, y, c, x))
        step *= 2
    return values


def on_device_general(
    tokens,
    cotangent,
    lengths,
    entry_weight,
    output_weight,
    gate_weight,
    down_weight,
    entry_first,
    output_first,
    gate_first,
    down_first,
    entry_second,
    output_second,
    gate_second,
    down_second,
    gains,
    gains_first,
    gains_second,
):
    seq_count = tokens.shape[0]
    local_len = tokens.shape[1]
    group_size = HEADS // KV_HEADS
    query_cols = HEADS * HEAD_DIM
    key_cols = KV_HEADS * HEAD_DIM
    scale = HEAD_DIM ** (-0.5)
    bf16 = jnp.bfloat16
    single_float = jnp.float32
    entry_low = entry_weight.astype(bf16)
    output_low = output_weight.astype(bf16)
    gate_low = gate_weight.astype(bf16)
    down_low = down_weight.astype(bf16)
    entry_weight_whole, output_weight_whole, gate_weight_whole, down_weight_whole = (
        lax.all_gather(entry_low, ("dp", "shard"), axis=0, tiled=True),
        lax.all_gather(output_low, ("dp", "shard"), axis=0, tiled=True),
        lax.all_gather(gate_low, ("dp", "shard"), axis=0, tiled=True),
        lax.all_gather(down_low, ("dp", "shard"), axis=0, tiled=True),
    )
    g_attn = gains[:D]
    g_mlp = gains[D : 2 * D]
    g_query = gains[2 * D : 2 * D + HEAD_DIM]
    g_key = gains[2 * D + HEAD_DIM :]
    positions = lax.axis_index("shard") * local_len + jnp.arange(local_len)
    cosine, sine = angles(positions)
    cos_four = cosine[None, :, None, :]
    sin_four = sine[None, :, None, :]
    live = positions[None, :] < lengths[:, None]
    inputs = tokens.astype(single_float)
    normed_one, factor_one = norm_rows(inputs, g_attn)
    normed_reduced = normed_one.astype(bf16)
    projected = jnp.dot(normed_reduced, entry_weight_whole, preferred_element_type=single_float)
    query_raw = projected[..., :query_cols].reshape(seq_count, local_len, HEADS, HEAD_DIM)
    key_raw = projected[..., query_cols : query_cols + key_cols].reshape(
        seq_count, local_len, KV_HEADS, HEAD_DIM
    )
    value_low = projected[..., query_cols + key_cols :].astype(bf16)
    query_normed, query_factor = norm_rows(query_raw, g_query)
    key_normed, key_factor = norm_rows(key_raw, g_key)
    query_rot = rotate(query_normed, cos_four, sin_four, 1.0).astype(bf16)
    key_rot = rotate(key_normed, cos_four, sin_four, 1.0).astype(bf16)
    query_grouped = query_rot.reshape(seq_count, local_len, KV_HEADS, group_size, HEAD_DIM)
    key_all, value_all = (
        lax.all_gather(
            key_rot.reshape(seq_count, local_len, key_cols), "shard", axis=1, tiled=True
        ),
        lax.all_gather(value_low, "shard", axis=1, tiled=True),
    )
    whole_len = key_all.shape[1]
    key_heads = key_all.reshape(seq_count, whole_len, KV_HEADS, HEAD_DIM)
    value_heads = value_all.reshape(seq_count, whole_len, KV_HEADS, HEAD_DIM)
    key_place = jnp.arange(whole_len)
    allowed = (key_place[None, None, :] <= positions[None, :, None]) & (
        key_place[None, None, :] < lengths[:, None, None]
    )
    raw = (
        jnp.einsum(
            "sqgrd,skgd->sgrqk", query_grouped, key_heads, preferred_element_type=single_float
        )
        * scale
    )
    scores = jnp.where(allowed[:, None, None], raw, NEG)
    probs = jax.nn.softmax(scores, axis=-1)
    probs_low = probs.astype(bf16)
    context = jnp.einsum(
        "sgrqk,skgd->sqgrd", probs_low, value_heads, preferred_element_type=single_float
    )
    context_reduced = context.reshape(seq_count, local_len, query_cols).astype(bf16)
    attended = jnp.dot(context_reduced, output_weight_whole, preferred_element_type=single_float)
    middle = inputs + attended
    normed_two, factor_two = norm_rows(middle, g_mlp)
    second_normed_reduced = normed_two.astype(bf16)
    both = jnp.dot(second_normed_reduced, gate_weight_whole, preferred_element_type=single_float)
    gate_val = both[..., :FF]
    up_val = both[..., FF:]
    sigmoid_val = jax.nn.sigmoid(gate_val)
    silu_val = gate_val * sigmoid_val
    hidden_reduced = (silu_val * up_val).astype(bf16)
    mlp_out = jnp.dot(hidden_reduced, down_weight_whole, preferred_element_type=single_float)
    block_out = jnp.where(live[..., None], middle + mlp_out, 0.0).astype(bf16)
    backward_reduced = jnp.where(live[..., None], cotangent, jnp.zeros_like(cotangent))
    down_gradient = jnp.einsum(
        "goj,gob->jb", hidden_reduced, backward_reduced, preferred_element_type=single_float
    )
    hidden_gradient = jnp.einsum(
        "bov,gv->bog", backward_reduced, down_weight_whole, preferred_element_type=single_float
    )
    d_gate = hidden_gradient * up_val * sigmoid_val * (1.0 + gate_val * (1.0 - sigmoid_val))
    d_up = hidden_gradient * silu_val
    combined_gradient = jnp.concatenate([d_gate, d_up], axis=-1).astype(bf16)
    gate_gradient = jnp.einsum(
        "mit,mib->tb", second_normed_reduced, combined_gradient, preferred_element_type=single_float
    )
    owned_gate, owned_down = reduce_pair(gate_gradient, down_gradient)
    second_normed_gradient = jnp.einsum(
        "nar,yr->nay", combined_gradient, gate_weight_whole, preferred_element_type=single_float
    )
    d_middle_norm, mlp_gain_terms = norm_back(middle, factor_two, g_mlp, second_normed_gradient)
    d_middle = backward_reduced.astype(single_float) + d_middle_norm
    attention_gradient_reduced = d_middle.astype(bf16)
    output_gradient = jnp.einsum(
        "czm,czr->mr",
        context_reduced,
        attention_gradient_reduced,
        preferred_element_type=single_float,
    )
    context_gradient = jnp.einsum(
        "xoj,gj->xog",
        attention_gradient_reduced,
        output_weight_whole,
        preferred_element_type=single_float,
    )
    d_context_low = context_gradient.astype(bf16).reshape(
        seq_count, local_len, KV_HEADS, group_size, HEAD_DIM
    )
    d_probs = jnp.einsum(
        "sqgrd,skgd->sgrqk", d_context_low, value_heads, preferred_element_type=single_float
    )
    d_scores = probs * (d_probs - jnp.sum(probs * d_probs, axis=-1, keepdims=True))
    d_scores_low = d_scores.astype(bf16)
    d_query_rot = (
        jnp.einsum(
            "sgrqk,skgd->sqgrd", d_scores_low, key_heads, preferred_element_type=single_float
        )
        * scale
    )
    d_key_all = (
        jnp.einsum(
            "sgrqk,sqgrd->skgd", d_scores_low, query_grouped, preferred_element_type=single_float
        )
        * scale
    )
    d_value_all = jnp.einsum(
        "sgrqk,sqgrd->skgd", probs_low, d_context_low, preferred_element_type=single_float
    )
    d_key_own, d_value_own = (
        lax.psum_scatter(
            d_key_all.reshape(seq_count, whole_len, key_cols).astype(jnp.bfloat16),
            "shard",
            scatter_dimension=1,
            tiled=True,
        ).astype(jnp.float32),
        lax.psum_scatter(
            d_value_all.reshape(seq_count, whole_len, key_cols).astype(jnp.bfloat16),
            "shard",
            scatter_dimension=1,
            tiled=True,
        ).astype(jnp.float32),
    )
    d_query_turned = rotate(
        d_query_rot.reshape(seq_count, local_len, HEADS, HEAD_DIM), cos_four, sin_four, -1.0
    )
    d_key_turned = rotate(
        d_key_own.reshape(seq_count, local_len, KV_HEADS, HEAD_DIM), cos_four, sin_four, -1.0
    )
    d_query_raw, query_gain_terms = norm_back(query_raw, query_factor, g_query, d_query_turned)
    d_key_raw, key_gain_terms = norm_back(key_raw, key_factor, g_key, d_key_turned)
    projected_gradient = jnp.concatenate(
        [
            d_query_raw.reshape(seq_count, local_len, query_cols),
            d_key_raw.reshape(seq_count, local_len, key_cols),
            d_value_own,
        ],
        axis=-1,
    ).astype(bf16)
    entry_gradient = jnp.einsum(
        "mit,mib->tb", normed_reduced, projected_gradient, preferred_element_type=single_float
    )
    owned_entry, owned_output = reduce_pair(entry_gradient, output_gradient)
    first_normed_gradient = jnp.einsum(
        "nar,yr->nay", projected_gradient, entry_weight_whole, preferred_element_type=single_float
    )
    d_inputs_norm, attn_gain_terms = norm_back(inputs, factor_one, g_attn, first_normed_gradient)
    token_grad = d_middle + d_inputs_norm
    gain_terms = jnp.concatenate(
        [
            jnp.sum(attn_gain_terms, axis=(0, 1)),
            jnp.sum(mlp_gain_terms, axis=(0, 1)),
            jnp.sum(query_gain_terms, axis=(0, 1, 2)),
            jnp.sum(key_gain_terms, axis=(0, 1, 2)),
        ]
    )
    grad_gains = lax.psum(gain_terms, ("dp", "shard"))
    new_entry, new_entry_first, new_entry_second = adam(
        entry_weight, entry_first, entry_second, owned_entry, RATE_MATRIX, DECAY
    )
    new_output, new_output_first, new_output_second = adam(
        output_weight, output_first, output_second, owned_output, RATE_OUTPUT, DECAY
    )
    new_gate, new_gate_first, new_gate_second = adam(
        gate_weight, gate_first, gate_second, owned_gate, RATE_MATRIX, DECAY
    )
    new_down, new_down_first, new_down_second = adam(
        down_weight, down_first, down_second, owned_down, RATE_MATRIX, DECAY
    )
    new_gains, new_gains_first, new_gains_second = adam(
        gains, gains_first, gains_second, grad_gains, RATE_GAIN, 0.0
    )
    return (
        block_out,
        token_grad,
        new_entry,
        new_entry_first,
        new_entry_second,
        new_output,
        new_output_first,
        new_output_second,
        new_gate,
        new_gate_first,
        new_gate_second,
        new_down,
        new_down_first,
        new_down_second,
        new_gains,
        new_gains_first,
        new_gains_second,
    )


VMEM_LIMIT = 40 * 2**20


def rope_rows(values, cosine, sine):
    return values * cosine + pltpu.roll(values, HEAD_DIM // 2, 1) * sine


def project_heads(normed, weight, first_block, turned_blocks, plain_blocks, cosine, sine, gain):
    slots, width = normed.shape
    wide = 2 * HEAD_DIM
    blocks = turned_blocks + plain_blocks

    def kernel(normed_ref, weight_ref, cos_ref, sin_ref, gain_ref, raw_ref, low_ref):
        step = pl.program_id(0)
        block = jnp.dot(normed_ref[...], weight_ref[...], preferred_element_type=jnp.float32)

        def plain():
            low_ref[...] = block.astype(jnp.bfloat16)

        def turned():
            raw_ref[...] = block
            for head in range(2):
                part = block[:, head * HEAD_DIM : (head + 1) * HEAD_DIM]
                factor = lax.rsqrt(jnp.mean(part * part, axis=-1, keepdims=True) + EPS)
                rows = rope_rows(part * factor * gain_ref[...], cos_ref[...], sin_ref[...])
                low_ref[:, head * HEAD_DIM : (head + 1) * HEAD_DIM] = rows.astype(jnp.bfloat16)

        if plain_blocks:
            pl.when(step >= turned_blocks)(plain)
            pl.when(step < turned_blocks)(turned)
        else:
            turned()

    return pl.pallas_call(
        kernel,
        grid=(blocks,),
        out_shape=(
            jax.ShapeDtypeStruct((slots, turned_blocks * wide), jnp.float32),
            jax.ShapeDtypeStruct((slots, blocks * wide), jnp.bfloat16),
        ),
        in_specs=[
            pl.BlockSpec((slots, width), lambda j: (0, 0)),
            pl.BlockSpec((width, wide), lambda j: (0, first_block + j)),
            pl.BlockSpec((slots, HEAD_DIM), lambda j: (0, 0)),
            pl.BlockSpec((slots, HEAD_DIM), lambda j: (0, 0)),
            pl.BlockSpec((1, HEAD_DIM), lambda j: (0, 0)),
        ],
        out_specs=(
            pl.BlockSpec((slots, wide), lambda j: (0, jnp.minimum(j, turned_blocks - 1))),
            pl.BlockSpec((slots, wide), lambda j: (0, j)),
        ),
        compiler_params=pltpu.CompilerParams(vmem_limit_bytes=VMEM_LIMIT),
        cost_estimate=pl.CostEstimate(
            flops=8 * slots * width * blocks * wide,
            bytes_accessed=12 * 2**20,
            transcendentals=0,
        ),
        name="project_heads",
    )(normed, weight, cosine, sine, gain)


def masked_weights(query, key, places, span, shard, length, own):
    scores = lax.dot_general(
        query, key, (((1,), (1,)), ((), ())), preferred_element_type=jnp.float32
    ) * (HEAD_DIM ** (-0.5))
    slot, key_slot = places
    if own:
        allowed = (key_slot <= slot) & (key_slot + shard * span < length)
    else:
        allowed = (key_slot + (shard - 1) * span < length) & (shard > 0)
    return jnp.where(allowed, jnp.exp(scores), 0.0)


def attend(query, low, other, lengths, shard, seqs, span):
    slots = seqs * span
    wide = 2 * HEAD_DIM

    def kernel(len_ref, place_ref, query_ref, key_ref, value_ref, key_far, value_far, out_ref):
        length, here = len_ref[pl.program_id(0)], place_ref[0]
        places = [lax.broadcasted_iota(jnp.int32, (span, span), axis) for axis in (0, 1)]
        for head in range(2):
            query = query_ref[:, head * HEAD_DIM : (head + 1) * HEAD_DIM]
            near = masked_weights(query, key_ref[...], places, span, here, length, True)
            far = masked_weights(query, key_far[...], places, span, here, length, False)
            total = jnp.sum(near, axis=-1, keepdims=True) + jnp.sum(far, axis=-1, keepdims=True)
            inverse = 1.0 / total
            context = jnp.dot(
                (near * inverse).astype(jnp.bfloat16),
                value_ref[...],
                preferred_element_type=jnp.float32,
            ) + jnp.dot(
                (far * inverse).astype(jnp.bfloat16),
                value_far[...],
                preferred_element_type=jnp.float32,
            )
            out_ref[:, head * HEAD_DIM : (head + 1) * HEAD_DIM] = context.astype(jnp.bfloat16)

    block = lambda offset: pl.BlockSpec((span, HEAD_DIM), lambda s, g: (s, offset + g))
    return pl.pallas_call(
        kernel,
        grid=(seqs, KV_HEADS),
        out_shape=jax.ShapeDtypeStruct((slots, HEADS * HEAD_DIM), jnp.bfloat16),
        in_specs=[
            pl.BlockSpec(memory_space=pltpu.SMEM),
            pl.BlockSpec(memory_space=pltpu.SMEM),
            pl.BlockSpec((span, wide), lambda s, g: (s, g)),
            block(0),
            block(KV_HEADS),
            block(0),
            block(KV_HEADS),
        ],
        out_specs=pl.BlockSpec((span, wide), lambda s, g: (s, g)),
        compiler_params=pltpu.CompilerParams(vmem_limit_bytes=VMEM_LIMIT),
        cost_estimate=pl.CostEstimate(
            flops=8 * slots * span * HEADS * HEAD_DIM,
            bytes_accessed=12 * 2**20,
            transcendentals=2 * slots * span * HEADS,
        ),
        name="attend",
    )(lengths, shard, query, low, low, other, other)


def norm_back_rows(raw, gain, incoming):
    factor = lax.rsqrt(jnp.mean(raw * raw, axis=-1, keepdims=True) + EPS)
    normal = raw * factor
    scaled = incoming * gain
    inner = jnp.mean(scaled * normal, axis=-1, keepdims=True)
    return factor * (scaled - normal * inner), jnp.sum(incoming * normal, axis=0, keepdims=True)


def attend_back(
    query, low, other, raw, d_context, lengths, shard, cosine, sine, gain, seqs, span, after
):
    slots = seqs * span
    wide = 2 * HEAD_DIM
    scale = HEAD_DIM ** (-0.5)

    def kernel(
        len_ref,
        place_ref,
        query_ref,
        key_ref,
        value_ref,
        key_far,
        value_far,
        raw_ref,
        d_context_ref,
        cos_ref,
        sin_ref,
        gain_ref,
        *rest,
    ):
        d_query_ref, d_near_ref, d_value_ref, far_ref, far_value_ref, terms_ref = rest[-6:]
        length, here = len_ref[pl.program_id(0)], place_ref[0]
        places = [lax.broadcasted_iota(jnp.int32, (span, span), axis) for axis in (0, 1)]
        keys, values = (key_ref[...], key_far[...]), (value_ref[...], value_far[...])
        d_keys, d_values = [0.0, 0.0], [0.0, 0.0]
        terms = 0.0
        for head in range(2):
            cols = slice(head * HEAD_DIM, (head + 1) * HEAD_DIM)
            query, d_out = query_ref[:, cols], d_context_ref[:, cols]
            weights = [
                masked_weights(query, keys[i], places, span, here, length, i == 0)
                for i in range(2)
            ]
            total = sum(jnp.sum(w, axis=-1, keepdims=True) for w in weights)
            inverse = 1.0 / total
            probs = [w * inverse for w in weights]
            d_probs = [
                lax.dot_general(
                    d_out, values[i], (((1,), (1,)), ((), ())), preferred_element_type=jnp.float32
                )
                for i in range(2)
            ]
            inner = sum(jnp.sum(p * d, axis=-1, keepdims=True) for p, d in zip(probs, d_probs))
            d_query = 0.0
            for i in range(2):
                d_scores = (probs[i] * (d_probs[i] - inner)).astype(jnp.bfloat16)
                turn = (((0,), (0,)), ((), ()))
                d_query += jnp.dot(d_scores, keys[i], preferred_element_type=jnp.float32)
                d_keys[i] += lax.dot_general(
                    d_scores, query, turn, preferred_element_type=jnp.float32
                )
                d_values[i] += lax.dot_general(
                    probs[i].astype(jnp.bfloat16), d_out, turn, preferred_element_type=jnp.float32
                )
            turned = rope_rows(d_query * scale, cos_ref[...], -sin_ref[...])
            d_raw, gain_term = norm_back_rows(raw_ref[:, cols], gain_ref[...], turned)
            d_query_ref[:, cols] = d_raw.astype(jnp.bfloat16)
            terms += gain_term
        d_near_ref[...] = d_keys[0] * scale
        d_value_ref[...] = d_values[0]
        far_ref[...] = (d_keys[1] * scale).astype(jnp.bfloat16)
        far_value_ref[...] = d_values[1].astype(jnp.bfloat16)

        @pl.when((pl.program_id(0) == 0) & (pl.program_id(1) == 0))
        def _():
            terms_ref[...] = jnp.zeros_like(terms_ref)

        terms_ref[...] += terms

    block = lambda offset: pl.BlockSpec((span, HEAD_DIM), lambda s, g: (s, offset + g))
    pair = pl.BlockSpec((span, wide), lambda s, g: (s, g))
    table = pl.BlockSpec((span, HEAD_DIM), lambda s, g: (0, 0))
    key_shape = (slots, KV_HEADS * HEAD_DIM)
    return pl.pallas_call(
        kernel,
        grid=(seqs, KV_HEADS),
        out_shape=(
            jax.ShapeDtypeStruct((slots, HEADS * HEAD_DIM), jnp.bfloat16),
            jax.ShapeDtypeStruct(key_shape, jnp.float32),
            jax.ShapeDtypeStruct(key_shape, jnp.float32),
            jax.ShapeDtypeStruct(key_shape, jnp.bfloat16),
            jax.ShapeDtypeStruct(key_shape, jnp.bfloat16),
            jax.ShapeDtypeStruct((1, HEAD_DIM), jnp.float32),
        ),
        in_specs=[
            pl.BlockSpec(memory_space=pltpu.SMEM),
            pl.BlockSpec(memory_space=pltpu.SMEM),
            pair,
            block(0),
            block(KV_HEADS),
            block(0),
            block(KV_HEADS),
            pair,
            pair,
            table,
            table,
            pl.BlockSpec((1, HEAD_DIM), lambda s, g: (0, 0)),
        ]
        + [pl.BlockSpec(memory_space=pl.ANY)] * len(after),
        out_specs=(
            pair,
            block(0),
            block(0),
            block(0),
            block(0),
            pl.BlockSpec((1, HEAD_DIM), lambda s, g: (0, 0)),
        ),
        compiler_params=pltpu.CompilerParams(vmem_limit_bytes=VMEM_LIMIT),
        cost_estimate=pl.CostEstimate(
            flops=20 * slots * span * HEADS * HEAD_DIM,
            bytes_accessed=24 * 2**20,
            transcendentals=2 * slots * span * HEADS,
        ),
        name="attend_back",
    )(lengths, shard, query, low, low, other, other, raw, d_context, cosine, sine, gain, *after)


def key_value_back(raw, d_key, d_value, key_arrived, value_arrived, cosine, sine, gain, after):
    slots = raw.shape[0]

    def kernel(
        raw_ref, key_ref, value_ref, key_more, value_more, cos_ref, sin_ref, gain_ref, *rest
    ):
        out_ref, terms_ref = rest[-2:]
        key_cols = pl.ds(pl.multiple_of(pl.program_id(0) * HEAD_DIM, HEAD_DIM), HEAD_DIM)
        place = pl.multiple_of((KV_HEADS + pl.program_id(0)) * HEAD_DIM, HEAD_DIM)
        d_turned = key_ref[...] + key_more[...].astype(jnp.float32)
        turned = rope_rows(d_turned, cos_ref[...], -sin_ref[...])
        d_raw, gain_term = norm_back_rows(raw_ref[...], gain_ref[...], turned)
        out_ref[:, key_cols] = d_raw.astype(jnp.bfloat16)
        out_ref[:, pl.ds(place, HEAD_DIM)] = (value_ref[...] + value_more[...].astype(jnp.float32)).astype(
            jnp.bfloat16
        )

        @pl.when(pl.program_id(0) == 0)
        def _():
            terms_ref[...] = jnp.zeros_like(terms_ref)

        terms_ref[...] += gain_term

    block = lambda offset: pl.BlockSpec((slots, HEAD_DIM), lambda g: (0, offset + g))
    table = pl.BlockSpec((slots, HEAD_DIM), lambda g: (0, 0))
    row = pl.BlockSpec((1, HEAD_DIM), lambda g: (0, 0))
    both_cols = 2 * KV_HEADS * HEAD_DIM
    return pl.pallas_call(
        kernel,
        grid=(KV_HEADS,),
        out_shape=(
            jax.ShapeDtypeStruct((slots, both_cols), jnp.bfloat16),
            jax.ShapeDtypeStruct((1, HEAD_DIM), jnp.float32),
        ),
        in_specs=[block(0), block(0), block(0), block(0), block(0), table, table, row]
        + [pl.BlockSpec(memory_space=pl.ANY)] * len(after),
        out_specs=(pl.BlockSpec((slots, both_cols), lambda g: (0, 0)), row),
        compiler_params=pltpu.CompilerParams(vmem_limit_bytes=VMEM_LIMIT),
        cost_estimate=pl.CostEstimate(
            flops=20 * slots * KV_HEADS * HEAD_DIM, bytes_accessed=11 * 2**20, transcendentals=0
        ),
        name="key_value_back",
    )(raw, d_key, d_value, key_arrived, value_arrived, cosine, sine, gain, *after)


def on_device(
    tokens,
    cotangent,
    lengths,
    entry_weight,
    output_weight,
    gate_weight,
    down_weight,
    entry_first,
    output_first,
    gate_first,
    down_first,
    entry_second,
    output_second,
    gate_second,
    down_second,
    gains,
    gains_first,
    gains_second,
):
    seqs, span, width = tokens.shape
    replicas, members = lax.axis_size("dp"), lax.axis_size("shard")
    deep = replicas // 4
    rows_fit = all(
        w.shape[0] % 16 == 0 for w in (entry_weight, output_weight, gate_weight, down_weight)
    )
    if members != 2 or replicas % 8 or deep & (deep - 1) or not rows_fit:
        return on_device_general(
            tokens,
            cotangent,
            lengths,
            entry_weight,
            output_weight,
            gate_weight,
            down_weight,
            entry_first,
            output_first,
            gate_first,
            down_first,
            entry_second,
            output_second,
            gate_second,
            down_second,
            gains,
            gains_first,
            gains_second,
        )
    bf16, f32 = jnp.bfloat16, jnp.float32
    grid = Grid(replicas)
    slots = seqs * span
    query_cols = HEADS * HEAD_DIM
    gather_sc = lambda w: lax.all_gather(w.astype(bf16), ("dp", "shard"), axis=0, tiled=True)
    entry_whole, (column, first, second) = gather_rows(grid, entry_weight.astype(bf16))
    output_whole = gather_sc(output_weight)
    down_whole = gather_sc(down_weight)
    gate_whole, _ = gather_rows(
        grid, tie(gate_weight.astype(bf16), column), after_column=(first, second)
    )

    g_attn = gains[:D]
    g_mlp = gains[D : 2 * D]
    g_query = gains[2 * D : 2 * D + HEAD_DIM]
    g_key = gains[2 * D + HEAD_DIM :]
    positions = grid.x * span + jnp.arange(span)
    cosine, sine = angles(positions)
    cosine = jnp.concatenate([cosine, cosine], axis=1)
    sine = jnp.concatenate([-sine, sine], axis=1)
    cosine, sine = jnp.concatenate([cosine] * seqs), jnp.concatenate([sine] * seqs)
    live = (positions[None, :] < lengths[:, None]).reshape(slots, 1)
    shard = grid.x.reshape(1).astype(jnp.int32)

    def dot(left, right):
        return jnp.dot(left, right, preferred_element_type=f32)

    def dot_turned(left, right):
        return lax.dot_general(left, right, (((1,), (1,)), ((), ())), preferred_element_type=f32)

    inputs = tokens.astype(f32).reshape(slots, width)
    normed_one, factor_one = norm_rows(inputs, g_attn)
    normed_one_low = normed_one.astype(bf16)
    query_blocks, key_blocks = HEADS // 2, KV_HEADS // 2
    g_query, g_key = g_query.reshape(1, HEAD_DIM), g_key.reshape(1, HEAD_DIM)
    key_raw, low = project_heads(
        normed_one_low, entry_whole, query_blocks, key_blocks, key_blocks, cosine, sine, g_key
    )
    other = grid.up_x(low)
    query_raw, query = project_heads(
        normed_one_low, entry_whole, 0, query_blocks, 0, cosine, sine, g_query
    )
    context = attend(query, low, other, lengths, shard, seqs, span)

    middle = inputs + dot(context, output_whole)
    normed_two, factor_two = norm_rows(middle, g_mlp)
    normed_two_low = normed_two.astype(bf16)
    both = dot(normed_two_low, gate_whole)
    gate_val, up_val = both[:, :FF], both[:, FF:]
    sigmoid_val = jax.nn.sigmoid(gate_val)
    silu_val = gate_val * sigmoid_val
    hidden = (silu_val * up_val).astype(bf16)
    back = jnp.where(live, cotangent.reshape(slots, width), jnp.zeros((), bf16))
    down_part = both_cores(grid, hidden, *halves(grid, back))
    down_one, down_sent = scatter_one(grid, down_part)
    d_hidden = dot_turned(back, down_whole)
    d_gate = d_hidden * up_val * sigmoid_val * (1.0 + gate_val * (1.0 - sigmoid_val))
    d_up = d_hidden * silu_val
    d_both = jnp.concatenate([d_gate, d_up], axis=-1).astype(bf16)
    gate_part = both_cores(grid, normed_two_low, *halves(grid, d_both))
    gate_one, gate_sent = scatter_one(grid, gate_part)
    d_normed_two = dot_turned(d_both, gate_whole)
    d_middle_norm, mlp_gain_terms = norm_back(middle, factor_two, g_mlp, d_normed_two)
    d_middle = back.astype(f32) + d_middle_norm
    d_attended = d_middle.astype(bf16)
    d_context = dot_turned(d_attended, output_whole).astype(bf16)
    d_query, d_key, d_value, far_key, far_value, query_terms = attend_back(
        query,
        low,
        other,
        query_raw,
        d_context,
        lengths,
        shard,
        cosine,
        sine,
        g_query,
        seqs,
        span,
        (*down_sent, *gate_sent, *down_one),
    )
    key_arrived, value_arrived = grid.down_x(far_key), grid.down_x(far_value)
    down_two = scatter_two(grid, down_one)
    output_part = both_cores(grid, context, *halves(grid, d_attended))
    output_one, output_sent = scatter_one(grid, output_part, d_query)
    block_out = jnp.where(live, middle + dot(hidden, down_whole), 0.0).astype(bf16)
    d_key_value, key_terms = key_value_back(
        key_raw,
        d_key,
        d_value,
        key_arrived,
        value_arrived,
        cosine,
        sine,
        g_key,
        (*gate_one, down_two, *output_sent, block_out),
    )
    gate_two = scatter_two(grid, gate_one)
    output_two = scatter_two(grid, output_one)
    first_core = grid.c == 0
    entry_part = both_cores(
        grid,
        normed_one_low,
        jnp.where(first_core, d_query, d_key_value),
        jnp.where(first_core, d_key_value, d_query),
    )
    entry_one, entry_sent = scatter_one(grid, entry_part)
    entry_two = scatter_two(grid, entry_one)
    owned_down = scatter_three(grid, down_two)
    owned_gate = scatter_three(grid, gate_two)
    owned_output = scatter_three(grid, output_two)
    owned_entry = scatter_three(grid, entry_two)
    d_normed_one = dot_turned(d_query, entry_whole[:, :query_cols]) + dot_turned(
        d_key_value, entry_whole[:, query_cols:]
    )
    d_inputs_norm, attn_gain_terms = norm_back(inputs, factor_one, g_attn, d_normed_one)
    token_grad = (d_middle + d_inputs_norm).reshape(seqs, span, width)
    gain_terms = jnp.concatenate(
        [
            jnp.sum(attn_gain_terms, axis=0),
            jnp.sum(mlp_gain_terms, axis=0),
            query_terms[0],
            key_terms[0],
        ]
    )
    grad_gains = sum_all(grid, gain_terms.reshape(-1, HEAD_DIM)).reshape(-1)
    return (
        block_out.reshape(seqs, span, width),
        token_grad,
        *adam(entry_weight, entry_first, entry_second, owned_entry, RATE_MATRIX, DECAY),
        *adam(output_weight, output_first, output_second, owned_output, RATE_OUTPUT, DECAY),
        *adam(gate_weight, gate_first, gate_second, owned_gate, RATE_MATRIX, DECAY),
        *adam(down_weight, down_first, down_second, owned_down, RATE_MATRIX, DECAY),
        *adam(gains, gains_first, gains_second, grad_gains, RATE_GAIN, 0.0),
    )


def solution(mesh):
    return jax.shard_map(
        on_device,
        mesh=mesh,
        in_specs=(
            P("dp", "shard", None),
            P("dp", "shard", None),
            P("dp"),
            P(("dp", "shard"), None),
            P(("dp", "shard"), None),
            P(("dp", "shard"), None),
            P(("dp", "shard"), None),
            P(("dp", "shard"), None),
            P(("dp", "shard"), None),
            P(("dp", "shard"), None),
            P(("dp", "shard"), None),
            P(("dp", "shard"), None),
            P(("dp", "shard"), None),
            P(("dp", "shard"), None),
            P(("dp", "shard"), None),
            P(),
            P(),
            P(),
        ),
        out_specs=(
            P("dp", "shard", None),
            P("dp", "shard", None),
            P(("dp", "shard"), None),
            P(("dp", "shard"), None),
            P(("dp", "shard"), None),
            P(("dp", "shard"), None),
            P(("dp", "shard"), None),
            P(("dp", "shard"), None),
            P(("dp", "shard"), None),
            P(("dp", "shard"), None),
            P(("dp", "shard"), None),
            P(("dp", "shard"), None),
            P(("dp", "shard"), None),
            P(("dp", "shard"), None),
            P(),
            P(),
            P(),
        ),
        check_vma=False,
    )
```

```python
import jax
import jax.numpy as jnp
from jax import lax
from jax.experimental import pallas as pl
from jax.experimental.pallas import tpu as pltpu
from jax.sharding import PartitionSpec as P

D = 1024
HEADS = 16
KV_HEADS = 8
HEAD_DIM = 128
FF = 3072
STEP = 10


EPS = 1e-06
THETA = 1000000.0
NEG = -1e30
BETA_ONE = 0.9
BETA_TWO = 0.95
ADAM_EPS = 1e-08
DECAY = 0.1
RATE_MATRIX = 0.03
RATE_OUTPUT = 0.06
RATE_GAIN = 0.25


def norm_rows(values, gain):
    factor = lax.rsqrt(jnp.mean(values * values, axis=-1, keepdims=True) + EPS)
    return (values * factor * gain, factor)


def norm_back(values, factor, gain, incoming):
    normal = values * factor
    scaled = incoming * gain
    inner = jnp.mean(scaled * normal, axis=-1, keepdims=True)
    return (factor * (scaled - normal * inner), incoming * normal)


def rotate(values, cosine, sine, direction):
    half = values.shape[-1] // 2
    leading = values[..., :half]
    trailing = values[..., half:]
    return jnp.concatenate(
        [
            leading * cosine - direction * trailing * sine,
            trailing * cosine + direction * leading * sine,
        ],
        axis=-1,
    )


def angles(positions):
    freqs = THETA ** (-(jnp.arange(HEAD_DIM // 2).astype(jnp.float32) * 2.0) / HEAD_DIM)
    turned = positions.astype(jnp.float32)[:, None] * freqs[None, :]
    return (jnp.cos(turned), jnp.sin(turned))


def adam(weight, moment_one, moment_two, grad, rate, decay):
    new_one = BETA_ONE * moment_one + (1.0 - BETA_ONE) * grad
    new_two = BETA_TWO * moment_two + (1.0 - BETA_TWO) * grad * grad
    ratio = (
        new_one / (1.0 - BETA_ONE**STEP) / (jnp.sqrt(new_two / (1.0 - BETA_TWO**STEP)) + ADAM_EPS)
    )
    return (weight - rate * (ratio + decay * weight), new_one, new_two)


def reduce_pair(grad_left, grad_right):
    replicas = lax.axis_size("dp")
    members = lax.axis_size("shard")
    owners = replicas * members
    left_cols = grad_left.shape[1]
    right_cols = grad_right.shape[1]
    left_rows = grad_left.shape[0] // owners
    right_rows = grad_right.shape[0] // owners
    left_owned, right_owned = (
        lax.psum_scatter(grad_left.reshape(-1), ("dp", "shard"), scatter_dimension=0, tiled=True),
        lax.psum_scatter(grad_right.reshape(-1), ("dp", "shard"), scatter_dimension=0, tiled=True),
    )
    return (left_owned.reshape(left_rows, left_cols), right_owned.reshape(right_rows, right_cols))


class Grid:
    def __init__(self, replicas):
        self.deep = replicas // 4
        index = lax.axis_index("dp")
        self.z = index // 4
        self.y = (index // 2) % 2
        self.c = index % 2
        self.x = lax.axis_index("shard")
        self.places = jnp.stack([self.z, self.y, self.c, self.x]).astype(jnp.int32)

    def pairs(self, turn):
        places = [
            (z, y, c, x)
            for z in range(self.deep)
            for y in range(2)
            for c in range(2)
            for x in range(2)
        ]
        flat = lambda z, y, c, x: ((z * 2 + y) * 2 + c) * 2 + x
        return [(flat(*p), flat(*turn(*p))) for p in places]

    def send(self, values, turn):
        return lax.ppermute(values, ("dp", "shard"), self.pairs(turn))

    def over_x(self, values):
        return self.send(values, lambda z, y, c, x: (z, y, c, 1 - x))

    def over_y(self, values):
        return self.send(values, lambda z, y, c, x: (z, 1 - y, c, x))

    def over_core(self, values):
        return self.send(values, lambda z, y, c, x: (z, y, 1 - c, x))

    def along_z(self, values, step):
        return self.send(values, lambda z, y, c, x: ((z + step) % self.deep, y, c, x))


def pick(values, index, axis):
    return lax.dynamic_index_in_dim(values, index, axis, keepdims=False)


def place_blocks(grid, own, sibling, rows, cols, *after):
    deep = grid.deep
    half = deep // 2
    spans = [(0, deep, 0, 0), (0, deep, 0, 1), (0, deep, 1, 0), (0, half, 1, 1), (half, deep, 1, 1)]

    def kernel(place_ref, *refs):
        ins = refs[:10]
        out, held, sems, sent = refs[-4:]
        z, y, c, x = [place_ref[i] for i in range(4)]
        copies = []
        for core in range(2):
            for piece, (first, last, dy, dx) in enumerate(spans):
                for step in range(first, last):
                    zz = lax.rem(z - step + deep, deep)
                    yy = lax.rem(y + dy, 2)
                    cc = lax.rem(c + core, 2)
                    xx = lax.rem(x + dx, 2)
                    block = ((zz * 2 + yy) * 2 + cc) * 2 + xx
                    turn = len(copies)
                    copies.append(
                        (
                            pltpu.make_async_copy(
                                ins[core * 5 + piece].at[step - first],
                                held.at[turn],
                                sems.at[turn],
                            ),
                            pltpu.make_async_copy(held.at[turn], out.at[block], sent.at[turn]),
                        )
                    )
        for arrive, leave in copies:
            arrive.start()
        for arrive, leave in copies:
            arrive.wait()
            leave.start()
        for arrive, leave in copies:
            leave.wait()

    blocks = deep * 8
    whole = pl.pallas_call(
        kernel,
        out_shape=jax.ShapeDtypeStruct((blocks, rows, cols), jnp.bfloat16),
        in_specs=[pl.BlockSpec(memory_space=pltpu.SMEM)]
        + [pl.BlockSpec(memory_space=pl.ANY)] * (10 + len(after)),
        out_specs=pl.BlockSpec(memory_space=pl.ANY),
        scratch_shapes=[
            pltpu.VMEM((blocks, rows, cols), jnp.bfloat16),
            pltpu.SemaphoreType.DMA((blocks,)),
            pltpu.SemaphoreType.DMA((blocks,)),
        ],
        compiler_params=pltpu.CompilerParams(vmem_limit_bytes=blocks * rows * cols * 2 + 2**21),
        cost_estimate=pl.CostEstimate(
            flops=0, bytes_accessed=blocks * rows * cols * 4, transcendentals=0
        ),
        name="place_blocks",
    )(grid.places, *own, *sibling, *after)
    return whole.reshape(blocks * rows, cols)


def hold(values, *after):
    return tuple(tie(value, *after) for value in values)


def column_of(shard, moved):
    return jnp.stack([shard] + [moved[step] for step in sorted(moved)])


def gather_two(grid, column):
    return column, grid.over_x(column), grid.over_y(column)


def gather_sends(grid, columns, *after):
    half = grid.deep // 2
    return tie(columns[1][:half], *after), tie(columns[2][half:], *after)


def gather_three(grid, sends):
    return grid.over_y(sends[0]), grid.over_x(sends[1])


def gather_end(grid, columns, last, shape, *after):
    own = (*columns, *last)
    sibling = tuple(grid.over_core(piece) for piece in own)
    return place_blocks(grid, own, sibling, *shape, *after)


def far_half(grid, values):
    cols = values.shape[1] // 2
    return lax.dynamic_slice_in_dim(values, (1 - grid.c) * cols, cols, 1)


def tie(value, *after):
    if not after:
        return value

    def kernel(*refs):
        pass

    return pl.pallas_call(
        kernel,
        out_shape=jax.ShapeDtypeStruct(value.shape, value.dtype),
        in_specs=[pl.BlockSpec(memory_space=pl.ANY)] * (1 + len(after)),
        out_specs=pl.BlockSpec(memory_space=pl.ANY),
        input_output_aliases={0: 0},
        cost_estimate=pl.CostEstimate(flops=0, bytes_accessed=0, transcendentals=0),
        name="tie",
    )(value, *after)


def sum_blocks(grid, left, right, left_far, right_far, *after):
    deep = grid.deep
    slots, width = left.shape
    cols = right_far.shape[1]
    wide = width // (deep * 2)
    rows = wide // 4
    turned = (((0,), (0,)), ((), ()))

    def kernel(place, left_ref, left_more, right_ref, right_more, *rest):
        first_sent, first_kept, second_sent, second_kept = rest[-4:]
        step = pl.program_id(0)
        total = lax.dot_general(
            left_ref[...], right_ref[...], turned, preferred_element_type=jnp.float32
        ) + lax.dot_general(
            left_more[...], right_more[...], turned, preferred_element_type=jnp.float32
        )
        parts = [total[i * rows : (i + 1) * rows, :].astype(jnp.bfloat16) for i in range(4)]
        lower = place[3] == 0

        def put(ref):
            ref[0, 0] = jnp.where(lower, parts[1], parts[0])
            ref[1, 0] = jnp.where(lower, parts[0], parts[1])

        pl.when(step < deep)(lambda: put(first_sent))
        pl.when(step >= deep)(lambda: put(first_kept))
        second_sent[0, 0] = jnp.where(lower, parts[3], parts[2])
        second_kept[0, 0] = jnp.where(lower, parts[2], parts[3])

    def block(s, place):
        return (0, (s % deep) * 2 + jnp.where(s < deep, 1 - place[1], place[1]))

    shape = jax.ShapeDtypeStruct((2, deep, rows, cols), jnp.bfloat16)
    second = pl.BlockSpec((1, 1, rows, cols), lambda s, place: (s // deep, s % deep, 0, 0))
    return pl.pallas_call(
        kernel,
        grid_spec=pltpu.PrefetchScalarGridSpec(
            num_scalar_prefetch=1,
            grid=(2 * deep,),
            in_specs=[
                pl.BlockSpec((slots, wide), block),
                pl.BlockSpec((slots, wide), block),
                pl.BlockSpec((slots, cols), lambda s, place: (0, place[2])),
                pl.BlockSpec((slots, cols), lambda s, place: (0, 0)),
            ]
            + [pl.BlockSpec(memory_space=pl.ANY)] * len(after),
            out_specs=(
                pl.BlockSpec(
                    (2, 1, rows, cols), lambda s, place: (0, jnp.minimum(s, deep - 1), 0, 0)
                ),
                pl.BlockSpec(
                    (2, 1, rows, cols), lambda s, place: (0, jnp.maximum(s - deep, 0), 0, 0)
                ),
                second,
                second,
            ),
        ),
        out_shape=(shape,) * 4,
        compiler_params=pltpu.CompilerParams(vmem_limit_bytes=28 * 2**20),
        cost_estimate=pl.CostEstimate(
            flops=4 * slots * width * cols, bytes_accessed=16 * 2**20, transcendentals=0
        ),
        name="sum_blocks",
    )(grid.places, left, left_far, right, right_far, *after)


def added(left, right):
    return (left.astype(jnp.float32) + right.astype(jnp.float32)).astype(jnp.bfloat16)


def scatter_two(grid, parts, *after):
    first_sent, first_kept, second_sent, second_kept = parts
    first_more, second_more = grid.over_y(first_sent), grid.over_x(second_sent)
    _, deep, rows, cols = first_kept.shape

    def kernel(first, first_new, second, second_new, *rest):
        first_out, first_held, second_out, second_held = rest[-4:]
        first_out[...] = added(first[0], first_new[0])
        first_held[...] = added(first[1], first_new[1])
        second_out[...] = added(second[0], second_new[0])
        second_held[...] = added(second[1], second_new[1])

    pair = pl.BlockSpec((2, 1, rows, cols), lambda z: (0, z, 0, 0))
    out = pl.BlockSpec((1, rows, cols), lambda z: (z, 0, 0))
    shape = jax.ShapeDtypeStruct((deep, rows, cols), jnp.bfloat16)
    return pl.pallas_call(
        kernel,
        grid=(deep,),
        in_specs=[pair] * 4 + [pl.BlockSpec(memory_space=pl.ANY)] * len(after),
        out_specs=(out,) * 4,
        out_shape=(shape,) * 4,
        compiler_params=pltpu.CompilerParams(vmem_limit_bytes=12 * 2**20),
        cost_estimate=pl.CostEstimate(
            flops=4 * deep * rows * cols, bytes_accessed=24 * deep * rows * cols, transcendentals=0
        ),
        name="scatter_two",
    )(first_kept, first_more, second_kept, second_more, *after)


def scatter_three(grid, parts, *after):
    first_sent, first_kept, second_sent, second_kept = parts
    first_more, second_more = grid.over_x(first_sent), grid.over_y(second_sent)
    deep, rows, cols = first_kept.shape

    def kernel(place, first, first_new, second, second_new, *rest):
        outs = rest[-deep:]
        for step in range(deep):

            @pl.when(pl.program_id(0) == step)
            def _():
                outs[step][0] = added(first[0], first_new[0])
                outs[step][1] = added(second[0], second_new[0])

    part = pl.BlockSpec((1, rows, cols), lambda k, place: (lax.rem(place[0] + k, deep), 0, 0))
    return pl.pallas_call(
        kernel,
        grid_spec=pltpu.PrefetchScalarGridSpec(
            num_scalar_prefetch=1,
            grid=(deep,),
            in_specs=[part] * 4 + [pl.BlockSpec(memory_space=pl.ANY)] * len(after),
            out_specs=(pl.BlockSpec((2, rows, cols), lambda k, place: (0, 0, 0)),) * deep,
        ),
        out_shape=(jax.ShapeDtypeStruct((2, rows, cols), jnp.bfloat16),) * deep,
        compiler_params=pltpu.CompilerParams(vmem_limit_bytes=12 * 2**20),
        cost_estimate=pl.CostEstimate(
            flops=2 * deep * rows * cols, bytes_accessed=12 * deep * rows * cols, transcendentals=0
        ),
        name="scatter_three",
    )(grid.places, first_kept, first_more, second_kept, second_more, *after)


def along(grid, chip, total, steps, *after):
    total = tie(total, *after).astype(jnp.float32)
    for step in steps:
        total = total + grid.along_z(chip[step], step).astype(jnp.float32)
    return total


def scatter_end(grid, total):
    kept = pick(total, grid.c, 0)
    arrived = grid.over_core(pick(total, 1 - grid.c, 0))
    return jnp.where(
        grid.c == 0,
        jnp.concatenate([kept, arrived], axis=1),
        jnp.concatenate([arrived, kept], axis=1),
    )


def sum_plane(grid, values):
    values = values + grid.over_core(values)
    both = grid.send(values, lambda z, y, c, x: (z, 1 - y, c, 1 - x))
    return (values + grid.over_x(values)) + (grid.over_y(values) + both)


def sum_along(grid, values):
    step = 1
    while step < grid.deep:
        values = values + grid.send(values, lambda z, y, c, x: (z ^ step, y, c, x))
        step *= 2
    return values


def rope_rows(values, cosine, sine):
    return values * cosine + pltpu.roll(values, HEAD_DIM // 2, 1) * sine


def project_heads(normed, weight, cosine, sine, gains):
    slots, width = normed.shape
    cols = weight.shape[1]
    wide = 2 * HEAD_DIM
    query_blocks, turned_blocks = HEADS // 2, (HEADS + KV_HEADS) // 2

    def kernel(normed_ref, weight_ref, cos_ref, sin_ref, gain_ref, raw_ref, low_ref):
        step = pl.program_id(0)
        block = jnp.dot(normed_ref[...], weight_ref[...], preferred_element_type=jnp.float32)

        @pl.when(step >= turned_blocks)
        def _():
            low_ref[...] = block.astype(jnp.bfloat16)

        @pl.when(step < turned_blocks)
        def _():
            raw_ref[...] = block
            gain = jnp.where(step < query_blocks, gain_ref[0:1, :], gain_ref[1:2, :])
            for head in range(2):
                part = block[:, head * HEAD_DIM : (head + 1) * HEAD_DIM]
                factor = lax.rsqrt(jnp.mean(part * part, axis=-1, keepdims=True) + EPS)
                rows = rope_rows(part * factor * gain, cos_ref[...], sin_ref[...])
                low_ref[:, head * HEAD_DIM : (head + 1) * HEAD_DIM] = rows.astype(jnp.bfloat16)

    return pl.pallas_call(
        kernel,
        grid=(cols // wide,),
        out_shape=(
            jax.ShapeDtypeStruct((slots, turned_blocks * wide), jnp.float32),
            jax.ShapeDtypeStruct((slots, cols), jnp.bfloat16),
        ),
        in_specs=[
            pl.BlockSpec((slots, width), lambda j: (0, 0)),
            pl.BlockSpec((width, wide), lambda j: (0, j)),
            pl.BlockSpec((slots, HEAD_DIM), lambda j: (0, 0)),
            pl.BlockSpec((slots, HEAD_DIM), lambda j: (0, 0)),
            pl.BlockSpec((2, HEAD_DIM), lambda j: (0, 0)),
        ],
        out_specs=(
            pl.BlockSpec((slots, wide), lambda j: (0, jnp.minimum(j, turned_blocks - 1))),
            pl.BlockSpec((slots, wide), lambda j: (0, j)),
        ),
        compiler_params=pltpu.CompilerParams(vmem_limit_bytes=14 * 2**20),
        cost_estimate=pl.CostEstimate(
            flops=8 * slots * width * cols, bytes_accessed=24 * 2**20, transcendentals=0
        ),
        name="project_heads",
    )(normed, weight, cosine, sine, gains)


def masked_weights(query, key, turn, key_turn, length):
    scores = lax.dot_general(
        query, key, (((1,), (1,)), ((), ())), preferred_element_type=jnp.float32
    ) * (HEAD_DIM ** (-0.5))
    rows = scores.shape[0]
    key_slot = lax.broadcasted_iota(jnp.int32, scores.shape, 1)
    allowed = key_slot + key_turn * rows < length
    if turn == key_turn:
        allowed &= key_slot <= lax.broadcasted_iota(jnp.int32, scores.shape, 0)
    return jnp.where(allowed, jnp.exp(scores), 0.0)


def attend(low, length, after):
    slots = low.shape[0]
    half = slots // 2
    wide = 2 * HEAD_DIM

    def kernel(len_ref, query_ref, key_ref, value_ref, *rest):
        out_ref = rest[-1]
        for head in range(2):
            cols = slice(head * HEAD_DIM, (head + 1) * HEAD_DIM)
            for turn in range(2):
                rows = slice(turn * half, (turn + 1) * half)
                keys = [slice(i * half, (i + 1) * half) for i in range(turn + 1)]
                weights = [
                    masked_weights(query_ref[rows, cols], key_ref[k, :], turn, i, len_ref[0])
                    for i, k in enumerate(keys)
                ]
                inverse = 1.0 / sum(jnp.sum(w, axis=-1, keepdims=True) for w in weights)
                context = sum(
                    jnp.dot(
                        (w * inverse).astype(jnp.bfloat16),
                        value_ref[k, :],
                        preferred_element_type=jnp.float32,
                    )
                    for w, k in zip(weights, keys)
                )
                out_ref[rows, cols] = context.astype(jnp.bfloat16)

    block = lambda offset: pl.BlockSpec((slots, HEAD_DIM), lambda g: (0, offset + g))
    pair = pl.BlockSpec((slots, wide), lambda g: (0, g))
    return pl.pallas_call(
        kernel,
        grid=(KV_HEADS,),
        out_shape=jax.ShapeDtypeStruct((slots, HEADS * HEAD_DIM), jnp.bfloat16),
        in_specs=[
            pl.BlockSpec(memory_space=pltpu.SMEM),
            pair,
            block(HEADS),
            block(HEADS + KV_HEADS),
        ]
        + [pl.BlockSpec(memory_space=pl.ANY)] * len(after),
        out_specs=pair,
        compiler_params=pltpu.CompilerParams(vmem_limit_bytes=16 * 2**20),
        cost_estimate=pl.CostEstimate(
            flops=4 * slots * slots * HEADS * HEAD_DIM,
            bytes_accessed=24 * 2**20,
            transcendentals=2 * slots * slots * HEADS,
        ),
        name="attend",
    )(length, low, low, low, *after)


def norm_back_rows(raw, gain, incoming):
    factor = lax.rsqrt(jnp.mean(raw * raw, axis=-1, keepdims=True) + EPS)
    normal = raw * factor
    scaled = incoming * gain
    inner = jnp.mean(scaled * normal, axis=-1, keepdims=True)
    return factor * (scaled - normal * inner), jnp.sum(incoming * normal, axis=0, keepdims=True)


def attend_back(low, raw, d_context, length, cosine, sine, gains, after):
    slots = low.shape[0]
    half = slots // 2
    wide = 2 * HEAD_DIM
    scale = HEAD_DIM ** (-0.5)

    def kernel(
        len_ref,
        query_ref,
        key_ref,
        value_ref,
        raw_query_ref,
        raw_key_ref,
        d_context_ref,
        cos_ref,
        sin_ref,
        gain_ref,
        *rest,
    ):
        out_ref, terms_ref = rest[-2:]
        group = pl.program_id(0)
        halves = [slice(i * half, (i + 1) * half) for i in range(2)]
        keys, values = [key_ref[k, :] for k in halves], [value_ref[k, :] for k in halves]
        d_keys, d_values = [0.0, 0.0], [0.0, 0.0]
        query_terms, key_terms = 0.0, 0.0
        flip = (((0,), (0,)), ((), ()))
        for head in range(2):
            cols = slice(head * HEAD_DIM, (head + 1) * HEAD_DIM)
            for turn in range(2):
                rows = halves[turn]
                query, d_out = query_ref[rows, cols], d_context_ref[rows, cols]
                blocks = range(turn + 1)
                weights = [masked_weights(query, keys[i], turn, i, len_ref[0]) for i in blocks]
                inverse = 1.0 / sum(jnp.sum(w, axis=-1, keepdims=True) for w in weights)
                probs = [w * inverse for w in weights]
                d_probs = [
                    lax.dot_general(
                        d_out,
                        values[i],
                        (((1,), (1,)), ((), ())),
                        preferred_element_type=jnp.float32,
                    )
                    for i in blocks
                ]
                inner = sum(jnp.sum(p * d, axis=-1, keepdims=True) for p, d in zip(probs, d_probs))
                d_query = 0.0
                for i in blocks:
                    d_scores = (probs[i] * (d_probs[i] - inner)).astype(jnp.bfloat16)
                    d_query += jnp.dot(d_scores, keys[i], preferred_element_type=jnp.float32)
                    d_keys[i] += lax.dot_general(
                        d_scores, query, flip, preferred_element_type=jnp.float32
                    )
                    d_values[i] += lax.dot_general(
                        probs[i].astype(jnp.bfloat16),
                        d_out,
                        flip,
                        preferred_element_type=jnp.float32,
                    )
                turned = rope_rows(d_query * scale, cos_ref[rows, :], -sin_ref[rows, :])
                d_raw, term = norm_back_rows(raw_query_ref[rows, cols], gain_ref[0:1, :], turned)
                place = pl.multiple_of((2 * group + head) * HEAD_DIM, HEAD_DIM)
                out_ref[rows, pl.ds(place, HEAD_DIM)] = d_raw.astype(jnp.bfloat16)
                query_terms += term
        key_cols = pl.ds(pl.multiple_of((HEADS + group) * HEAD_DIM, HEAD_DIM), HEAD_DIM)
        place = pl.multiple_of((HEADS + KV_HEADS + group) * HEAD_DIM, HEAD_DIM)
        value_cols = pl.ds(place, HEAD_DIM)
        for i, rows in enumerate(halves):
            turned = rope_rows(d_keys[i] * scale, cos_ref[rows, :], -sin_ref[rows, :])
            d_raw, term = norm_back_rows(raw_key_ref[rows, :], gain_ref[1:2, :], turned)
            out_ref[rows, key_cols] = d_raw.astype(jnp.bfloat16)
            out_ref[rows, value_cols] = d_values[i].astype(jnp.bfloat16)
            key_terms += term

        @pl.when(group == 0)
        def _():
            terms_ref[...] = jnp.zeros_like(terms_ref)

        terms_ref[0:1, :] += query_terms
        terms_ref[1:2, :] += key_terms

    block = lambda offset: pl.BlockSpec((slots, HEAD_DIM), lambda g: (0, offset + g))
    pair = pl.BlockSpec((slots, wide), lambda g: (0, g))
    table = pl.BlockSpec((slots, HEAD_DIM), lambda g: (0, 0))
    all_cols = (HEADS + 2 * KV_HEADS) * HEAD_DIM
    return pl.pallas_call(
        kernel,
        grid=(KV_HEADS,),
        out_shape=(
            jax.ShapeDtypeStruct((slots, all_cols), jnp.bfloat16),
            jax.ShapeDtypeStruct((2, HEAD_DIM), jnp.float32),
        ),
        in_specs=[
            pl.BlockSpec(memory_space=pltpu.SMEM),
            pair,
            block(HEADS),
            block(HEADS + KV_HEADS),
            pair,
            block(HEADS),
            pair,
            table,
            table,
            pl.BlockSpec((2, HEAD_DIM), lambda g: (0, 0)),
        ]
        + [pl.BlockSpec(memory_space=pl.ANY)] * len(after),
        out_specs=(
            pl.BlockSpec((slots, all_cols), lambda g: (0, 0)),
            pl.BlockSpec((2, HEAD_DIM), lambda g: (0, 0)),
        ),
        compiler_params=pltpu.CompilerParams(vmem_limit_bytes=32 * 2**20),
        cost_estimate=pl.CostEstimate(
            flops=20 * slots * slots * HEADS * HEAD_DIM,
            bytes_accessed=48 * 2**20,
            transcendentals=2 * slots * slots * HEADS,
        ),
        name="attend_back",
    )(length, low, low, low, raw, raw, d_context, cosine, sine, gains, *after)


def whole_sequence(grid, values):
    kept, sent = pick(values, grid.x, 0), pick(values, 1 - grid.x, 0)
    arrived = grid.over_x(sent)
    return jnp.where(
        grid.x == 0, jnp.concatenate([kept, arrived]), jnp.concatenate([arrived, kept])
    )


def half_sequences(grid, values, way, *after):
    halves = values.reshape(2, values.shape[0] // 2, values.shape[1])
    kept, sent = pick(halves, grid.x, 0), tie(pick(halves, 1 - grid.x, 0), *after)
    arrived = grid.over_x(sent.astype(way)).astype(values.dtype)
    return jnp.where(grid.x == 0, jnp.stack([kept, arrived]), jnp.stack([arrived, kept]))


def on_device_general(
    tokens,
    cotangent,
    lengths,
    entry_weight,
    output_weight,
    gate_weight,
    down_weight,
    entry_first,
    output_first,
    gate_first,
    down_first,
    entry_second,
    output_second,
    gate_second,
    down_second,
    gains,
    gains_first,
    gains_second,
):
    seq_count = tokens.shape[0]
    local_len = tokens.shape[1]
    group_size = HEADS // KV_HEADS
    query_cols = HEADS * HEAD_DIM
    key_cols = KV_HEADS * HEAD_DIM
    scale = HEAD_DIM ** (-0.5)
    bf16 = jnp.bfloat16
    single_float = jnp.float32
    entry_low = entry_weight.astype(bf16)
    output_low = output_weight.astype(bf16)
    gate_low = gate_weight.astype(bf16)
    down_low = down_weight.astype(bf16)
    entry_weight_whole, output_weight_whole, gate_weight_whole, down_weight_whole = (
        lax.all_gather(entry_low, ("dp", "shard"), axis=0, tiled=True),
        lax.all_gather(output_low, ("dp", "shard"), axis=0, tiled=True),
        lax.all_gather(gate_low, ("dp", "shard"), axis=0, tiled=True),
        lax.all_gather(down_low, ("dp", "shard"), axis=0, tiled=True),
    )
    g_attn = gains[:D]
    g_mlp = gains[D : 2 * D]
    g_query = gains[2 * D : 2 * D + HEAD_DIM]
    g_key = gains[2 * D + HEAD_DIM :]
    positions = lax.axis_index("shard") * local_len + jnp.arange(local_len)
    cosine, sine = angles(positions)
    cos_four = cosine[None, :, None, :]
    sin_four = sine[None, :, None, :]
    live = positions[None, :] < lengths[:, None]
    inputs = tokens.astype(single_float)
    normed_one, factor_one = norm_rows(inputs, g_attn)
    normed_reduced = normed_one.astype(bf16)
    projected = jnp.dot(normed_reduced, entry_weight_whole, preferred_element_type=single_float)
    query_raw = projected[..., :query_cols].reshape(seq_count, local_len, HEADS, HEAD_DIM)
    key_raw = projected[..., query_cols : query_cols + key_cols].reshape(
        seq_count, local_len, KV_HEADS, HEAD_DIM
    )
    value_low = projected[..., query_cols + key_cols :].astype(bf16)
    query_normed, query_factor = norm_rows(query_raw, g_query)
    key_normed, key_factor = norm_rows(key_raw, g_key)
    query_rot = rotate(query_normed, cos_four, sin_four, 1.0).astype(bf16)
    key_rot = rotate(key_normed, cos_four, sin_four, 1.0).astype(bf16)
    query_grouped = query_rot.reshape(seq_count, local_len, KV_HEADS, group_size, HEAD_DIM)
    key_all, value_all = (
        lax.all_gather(
            key_rot.reshape(seq_count, local_len, key_cols), "shard", axis=1, tiled=True
        ),
        lax.all_gather(value_low, "shard", axis=1, tiled=True),
    )
    whole_len = key_all.shape[1]
    key_heads = key_all.reshape(seq_count, whole_len, KV_HEADS, HEAD_DIM)
    value_heads = value_all.reshape(seq_count, whole_len, KV_HEADS, HEAD_DIM)
    key_place = jnp.arange(whole_len)
    allowed = (key_place[None, None, :] <= positions[None, :, None]) & (
        key_place[None, None, :] < lengths[:, None, None]
    )
    raw = (
        jnp.einsum(
            "sqgrd,skgd->sgrqk", query_grouped, key_heads, preferred_element_type=single_float
        )
        * scale
    )
    scores = jnp.where(allowed[:, None, None], raw, NEG)
    probs = jax.nn.softmax(scores, axis=-1)
    probs_low = probs.astype(bf16)
    context = jnp.einsum(
        "sgrqk,skgd->sqgrd", probs_low, value_heads, preferred_element_type=single_float
    )
    context_reduced = context.reshape(seq_count, local_len, query_cols).astype(bf16)
    attended = jnp.dot(context_reduced, output_weight_whole, preferred_element_type=single_float)
    middle = inputs + attended
    normed_two, factor_two = norm_rows(middle, g_mlp)
    second_normed_reduced = normed_two.astype(bf16)
    both = jnp.dot(second_normed_reduced, gate_weight_whole, preferred_element_type=single_float)
    gate_val = both[..., :FF]
    up_val = both[..., FF:]
    sigmoid_val = jax.nn.sigmoid(gate_val)
    silu_val = gate_val * sigmoid_val
    hidden_reduced = (silu_val * up_val).astype(bf16)
    mlp_out = jnp.dot(hidden_reduced, down_weight_whole, preferred_element_type=single_float)
    block_out = jnp.where(live[..., None], middle + mlp_out, 0.0).astype(bf16)
    backward_reduced = jnp.where(live[..., None], cotangent, jnp.zeros_like(cotangent))
    down_gradient = jnp.einsum(
        "goj,gob->jb", hidden_reduced, backward_reduced, preferred_element_type=single_float
    )
    hidden_gradient = jnp.einsum(
        "bov,gv->bog", backward_reduced, down_weight_whole, preferred_element_type=single_float
    )
    d_gate = hidden_gradient * up_val * sigmoid_val * (1.0 + gate_val * (1.0 - sigmoid_val))
    d_up = hidden_gradient * silu_val
    combined_gradient = jnp.concatenate([d_gate, d_up], axis=-1).astype(bf16)
    gate_gradient = jnp.einsum(
        "mit,mib->tb", second_normed_reduced, combined_gradient, preferred_element_type=single_float
    )
    owned_gate, owned_down = reduce_pair(gate_gradient, down_gradient)
    second_normed_gradient = jnp.einsum(
        "nar,yr->nay", combined_gradient, gate_weight_whole, preferred_element_type=single_float
    )
    d_middle_norm, mlp_gain_terms = norm_back(middle, factor_two, g_mlp, second_normed_gradient)
    d_middle = backward_reduced.astype(single_float) + d_middle_norm
    attention_gradient_reduced = d_middle.astype(bf16)
    output_gradient = jnp.einsum(
        "czm,czr->mr",
        context_reduced,
        attention_gradient_reduced,
        preferred_element_type=single_float,
    )
    context_gradient = jnp.einsum(
        "xoj,gj->xog",
        attention_gradient_reduced,
        output_weight_whole,
        preferred_element_type=single_float,
    )
    d_context_low = context_gradient.astype(bf16).reshape(
        seq_count, local_len, KV_HEADS, group_size, HEAD_DIM
    )
    d_probs = jnp.einsum(
        "sqgrd,skgd->sgrqk", d_context_low, value_heads, preferred_element_type=single_float
    )
    d_scores = probs * (d_probs - jnp.sum(probs * d_probs, axis=-1, keepdims=True))
    d_scores_low = d_scores.astype(bf16)
    d_query_rot = (
        jnp.einsum(
            "sgrqk,skgd->sqgrd", d_scores_low, key_heads, preferred_element_type=single_float
        )
        * scale
    )
    d_key_all = (
        jnp.einsum(
            "sgrqk,sqgrd->skgd", d_scores_low, query_grouped, preferred_element_type=single_float
        )
        * scale
    )
    d_value_all = jnp.einsum(
        "sgrqk,sqgrd->skgd", probs_low, d_context_low, preferred_element_type=single_float
    )
    d_key_own, d_value_own = (
        lax.psum_scatter(
            d_key_all.reshape(seq_count, whole_len, key_cols).astype(jnp.bfloat16),
            "shard",
            scatter_dimension=1,
            tiled=True,
        ).astype(jnp.float32),
        lax.psum_scatter(
            d_value_all.reshape(seq_count, whole_len, key_cols).astype(jnp.bfloat16),
            "shard",
            scatter_dimension=1,
            tiled=True,
        ).astype(jnp.float32),
    )
    d_query_turned = rotate(
        d_query_rot.reshape(seq_count, local_len, HEADS, HEAD_DIM), cos_four, sin_four, -1.0
    )
    d_key_turned = rotate(
        d_key_own.reshape(seq_count, local_len, KV_HEADS, HEAD_DIM), cos_four, sin_four, -1.0
    )
    d_query_raw, query_gain_terms = norm_back(query_raw, query_factor, g_query, d_query_turned)
    d_key_raw, key_gain_terms = norm_back(key_raw, key_factor, g_key, d_key_turned)
    projected_gradient = jnp.concatenate(
        [
            d_query_raw.reshape(seq_count, local_len, query_cols),
            d_key_raw.reshape(seq_count, local_len, key_cols),
            d_value_own,
        ],
        axis=-1,
    ).astype(bf16)
    entry_gradient = jnp.einsum(
        "mit,mib->tb", normed_reduced, projected_gradient, preferred_element_type=single_float
    )
    owned_entry, owned_output = reduce_pair(entry_gradient, output_gradient)
    first_normed_gradient = jnp.einsum(
        "nar,yr->nay", projected_gradient, entry_weight_whole, preferred_element_type=single_float
    )
    d_inputs_norm, attn_gain_terms = norm_back(inputs, factor_one, g_attn, first_normed_gradient)
    token_grad = d_middle + d_inputs_norm
    gain_terms = jnp.concatenate(
        [
            jnp.sum(attn_gain_terms, axis=(0, 1)),
            jnp.sum(mlp_gain_terms, axis=(0, 1)),
            jnp.sum(query_gain_terms, axis=(0, 1, 2)),
            jnp.sum(key_gain_terms, axis=(0, 1, 2)),
        ]
    )
    grad_gains = lax.psum(gain_terms, ("dp", "shard"))
    new_entry, new_entry_first, new_entry_second = adam(
        entry_weight, entry_first, entry_second, owned_entry, RATE_MATRIX, DECAY
    )
    new_output, new_output_first, new_output_second = adam(
        output_weight, output_first, output_second, owned_output, RATE_OUTPUT, DECAY
    )
    new_gate, new_gate_first, new_gate_second = adam(
        gate_weight, gate_first, gate_second, owned_gate, RATE_MATRIX, DECAY
    )
    new_down, new_down_first, new_down_second = adam(
        down_weight, down_first, down_second, owned_down, RATE_MATRIX, DECAY
    )
    new_gains, new_gains_first, new_gains_second = adam(
        gains, gains_first, gains_second, grad_gains, RATE_GAIN, 0.0
    )
    return (
        block_out,
        token_grad,
        new_entry,
        new_entry_first,
        new_entry_second,
        new_output,
        new_output_first,
        new_output_second,
        new_gate,
        new_gate_first,
        new_gate_second,
        new_down,
        new_down_first,
        new_down_second,
        new_gains,
        new_gains_first,
        new_gains_second,
    )


def on_device(
    tokens,
    cotangent,
    lengths,
    entry_weight,
    output_weight,
    gate_weight,
    down_weight,
    entry_first,
    output_first,
    gate_first,
    down_first,
    entry_second,
    output_second,
    gate_second,
    down_second,
    gains,
    gains_first,
    gains_second,
):
    seqs, span, width = tokens.shape
    replicas, members = lax.axis_size("dp"), lax.axis_size("shard")
    deep = replicas // 4
    rows_fit = all(
        w.shape[0] % 16 == 0 for w in (entry_weight, output_weight, gate_weight, down_weight)
    )
    if members != 2 or replicas % 8 or deep & (deep - 1) or not rows_fit:
        return on_device_general(
            tokens,
            cotangent,
            lengths,
            entry_weight,
            output_weight,
            gate_weight,
            down_weight,
            entry_first,
            output_first,
            gate_first,
            down_first,
            entry_second,
            output_second,
            gate_second,
            down_second,
            gains,
            gains_first,
            gains_second,
        )
    bf16, f32 = jnp.bfloat16, jnp.float32
    grid = Grid(replicas)
    slots = seqs * span
    query_cols = HEADS * HEAD_DIM
    entry_low, output_low, gate_low, down_low = [
        w.astype(bf16) for w in (entry_weight, output_weight, gate_weight, down_weight)
    ]
    steps = range(1, deep)
    entry_column = column_of(entry_low, {s: grid.along_z(entry_low, s) for s in steps})
    inputs_low = whole_sequence(grid, tokens)

    output_whole = lax.all_gather(output_low, ("dp", "shard"), axis=0, tiled=True)
    gate_low, down_low = hold((gate_low, down_low), entry_column)
    gate_whole = lax.all_gather(gate_low, ("dp", "shard"), axis=0, tiled=True)
    entry_columns = gather_two(grid, entry_column)
    down_column = column_of(down_low, {s: grid.along_z(down_low, s) for s in steps})

    entry_sends = gather_sends(grid, entry_columns, down_column)
    entry_last = gather_three(grid, entry_sends)

    down_column = tie(down_column, *entry_last, inputs_low)
    down_columns = gather_two(grid, down_column)
    entry_whole = gather_end(grid, entry_columns, entry_last, entry_low.shape, down_column)

    g_attn = gains[:D]
    g_mlp = gains[D : 2 * D]
    g_heads = gains[2 * D :].reshape(2, HEAD_DIM)
    cosine, sine = angles(jnp.arange(slots))
    cosine = jnp.concatenate([cosine, cosine], axis=1)
    sine = jnp.concatenate([-sine, sine], axis=1)
    length = lax.dynamic_slice_in_dim(lengths, grid.x, 1)
    live = (jnp.arange(slots) < length[0]).reshape(slots, 1)

    def dot(left, right):
        return jnp.dot(left, right, preferred_element_type=f32)

    def dot_turned(left, right):
        return lax.dot_general(left, right, (((1,), (1,)), ((), ())), preferred_element_type=f32)

    inputs = inputs_low.astype(f32)
    normed_one, factor_one = norm_rows(inputs, g_attn)
    normed_one_low = normed_one.astype(bf16)
    raw, low = project_heads(normed_one_low, entry_whole, cosine, sine, g_heads)

    context = attend(low, length, (down_column,))
    down_sends = gather_sends(grid, down_columns, context)
    down_last = gather_three(grid, down_sends)
    back = whole_sequence(grid, tie(cotangent, *down_sends))
    back = jnp.where(live, back, jnp.zeros((), bf16))
    middle = inputs + dot(context, output_whole)
    normed_two, factor_two = norm_rows(middle, g_mlp)
    normed_two_low = normed_two.astype(bf16)
    down_whole = gather_end(grid, down_columns, down_last, down_low.shape, normed_two_low)
    both = dot(normed_two_low, gate_whole)
    gate_val, up_val = both[:, :FF], both[:, FF:]
    sigmoid_val = jax.nn.sigmoid(gate_val)
    silu_val = gate_val * sigmoid_val
    hidden = (silu_val * up_val).astype(bf16)
    hidden_far = grid.over_core(hidden)
    back_far = grid.over_core(far_half(grid, back))
    d_hidden = dot_turned(back, down_whole)
    d_gate = d_hidden * up_val * sigmoid_val * (1.0 + gate_val * (1.0 - sigmoid_val))
    d_up = d_hidden * silu_val
    d_both = jnp.concatenate([d_gate, d_up], axis=-1).astype(bf16)

    d_both = tie(d_both, hidden_far, back_far)
    down_one = sum_blocks(grid, hidden, back, hidden_far, back_far)
    both_far = grid.over_core(far_half(grid, d_both))
    normed_far = grid.over_core(normed_two_low)
    gate_one = sum_blocks(grid, normed_two_low, d_both, normed_far, both_far, *down_one)
    down_two = scatter_two(grid, down_one, *gate_one)

    d_normed_two = dot_turned(tie(d_both, *down_two), gate_whole)
    d_middle_norm, mlp_gain_terms = norm_back(middle, factor_two, g_mlp, d_normed_two)
    d_middle = back.astype(f32) + d_middle_norm
    d_attended = d_middle.astype(bf16)
    context_far = grid.over_core(tie(context, d_both))
    attended_far = grid.over_core(far_half(grid, d_attended))
    d_context = dot_turned(d_attended, output_whole).astype(bf16)
    output_one = sum_blocks(
        grid, context, d_attended, context_far, attended_far, *gate_one, *down_two, d_context
    )
    gate_two = scatter_two(grid, gate_one, *output_one)
    down_chip = scatter_three(grid, down_two, *gate_two)
    normed_one_far = grid.over_core(tie(normed_one_low, d_both))

    d_projected, head_terms = attend_back(
        low,
        raw,
        d_context,
        length,
        cosine,
        sine,
        g_heads,
        (*gate_two, *down_chip, *output_one, normed_one_far),
    )
    far_steps = [s for s in steps if s == deep // 2]
    near_steps = [s for s in steps if s != deep // 2]
    output_two = scatter_two(grid, output_one, d_projected)
    gate_chip = scatter_three(grid, gate_two, *output_two)
    d_projected = tie(d_projected, *gate_chip)
    projected_far = grid.over_core(far_half(grid, d_projected))
    entry_one = sum_blocks(grid, normed_one_low, d_projected, normed_one_far, projected_far)

    down_total = along(grid, down_chip, down_chip[0], steps, *entry_one)
    owned_down = scatter_end(grid, down_total)
    gate_total = along(grid, gate_chip, gate_chip[0], near_steps, *entry_one)
    output_chip = scatter_three(grid, output_two, *entry_one)
    d_projected = tie(d_projected, *entry_one, *output_chip, gate_total)
    d_normed_one = dot_turned(d_projected, entry_whole)
    d_inputs_norm, attn_gain_terms = norm_back(inputs, factor_one, g_attn, d_normed_one)
    token_grad = d_middle + d_inputs_norm
    gain_terms = jnp.concatenate(
        [jnp.sum(attn_gain_terms, axis=0), jnp.sum(mlp_gain_terms, axis=0), head_terms.reshape(-1)]
    )
    gain_sums = sum_plane(grid, gain_terms.reshape(-1, HEAD_DIM))

    entry_two = scatter_two(grid, entry_one, gain_sums, token_grad, owned_down)
    block_out = middle + dot(tie(hidden, *entry_two), down_whole)
    block_out = jnp.where(live, block_out, 0.0).astype(bf16)
    gate_total = along(grid, gate_chip, gate_total, far_steps, block_out)
    block_out = half_sequences(grid, block_out, bf16, *entry_two)
    token_grad = half_sequences(grid, token_grad, bf16, *entry_two)
    owned_gate = scatter_end(grid, gate_total)
    output_total = along(grid, output_chip, output_chip[0], steps, *entry_two)
    owned_output = scatter_end(grid, output_total)
    grad_gains = sum_along(grid, tie(gain_sums, *entry_two)).reshape(-1)
    made_output = adam(output_weight, output_first, output_second, owned_output, RATE_OUTPUT, DECAY)
    made_gate = adam(gate_weight, gate_first, gate_second, owned_gate, RATE_MATRIX, DECAY)
    made_down = adam(down_weight, down_first, down_second, owned_down, RATE_MATRIX, DECAY)

    entry_chip = scatter_three(grid, entry_two, made_output[0], made_gate[0], made_down[0], grad_gains)
    entry_total = along(grid, entry_chip, entry_chip[0], steps, block_out, token_grad)
    owned_entry = scatter_end(grid, entry_total)
    return (
        block_out,
        token_grad,
        *adam(entry_weight, entry_first, entry_second, owned_entry, RATE_MATRIX, DECAY),
        *made_output,
        *made_gate,
        *made_down,
        *adam(gains, gains_first, gains_second, grad_gains, RATE_GAIN, 0.0),
    )


def solution(mesh):
    return jax.shard_map(
        on_device,
        mesh=mesh,
        in_specs=(
            P("dp", "shard", None),
            P("dp", "shard", None),
            P("dp"),
            P(("dp", "shard"), None),
            P(("dp", "shard"), None),
            P(("dp", "shard"), None),
            P(("dp", "shard"), None),
            P(("dp", "shard"), None),
            P(("dp", "shard"), None),
            P(("dp", "shard"), None),
            P(("dp", "shard"), None),
            P(("dp", "shard"), None),
            P(("dp", "shard"), None),
            P(("dp", "shard"), None),
            P(("dp", "shard"), None),
            P(),
            P(),
            P(),
        ),
        out_specs=(
            P("dp", "shard", None),
            P("dp", "shard", None),
            P(("dp", "shard"), None),
            P(("dp", "shard"), None),
            P(("dp", "shard"), None),
            P(("dp", "shard"), None),
            P(("dp", "shard"), None),
            P(("dp", "shard"), None),
            P(("dp", "shard"), None),
            P(("dp", "shard"), None),
            P(("dp", "shard"), None),
            P(("dp", "shard"), None),
            P(("dp", "shard"), None),
            P(("dp", "shard"), None),
            P(),
            P(),
            P(),
        ),
        check_vma=False,
    )
```

```python
import jax
import jax.numpy as jnp
from jax import lax
from jax.experimental import pallas as pl
from jax.experimental.pallas import tpu as pltpu
from jax.sharding import PartitionSpec as P

D = 1024
HEADS = 16
KV_HEADS = 8
HEAD_DIM = 128
FF = 3072
STEP = 10


EPS = 1e-06
THETA = 1000000.0
NEG = -1e30
BETA_ONE = 0.9
BETA_TWO = 0.95
ADAM_EPS = 1e-08
DECAY = 0.1
RATE_MATRIX = 0.03
RATE_OUTPUT = 0.06
RATE_GAIN = 0.25


def norm_rows(values, gain):
    factor = lax.rsqrt(jnp.mean(values * values, axis=-1, keepdims=True) + EPS)
    return (values * factor * gain, factor)


def norm_back(values, factor, gain, incoming):
    normal = values * factor
    scaled = incoming * gain
    inner = jnp.mean(scaled * normal, axis=-1, keepdims=True)
    return (factor * (scaled - normal * inner), incoming * normal)


def rotate(values, cosine, sine, direction):
    half = values.shape[-1] // 2
    leading = values[..., :half]
    trailing = values[..., half:]
    return jnp.concatenate(
        [
            leading * cosine - direction * trailing * sine,
            trailing * cosine + direction * leading * sine,
        ],
        axis=-1,
    )


def angles(positions):
    freqs = THETA ** (-(jnp.arange(HEAD_DIM // 2).astype(jnp.float32) * 2.0) / HEAD_DIM)
    turned = positions.astype(jnp.float32)[:, None] * freqs[None, :]
    return (jnp.cos(turned), jnp.sin(turned))


def adam(weight, moment_one, moment_two, grad, rate, decay):
    new_one = BETA_ONE * moment_one + (1.0 - BETA_ONE) * grad
    new_two = BETA_TWO * moment_two + (1.0 - BETA_TWO) * grad * grad
    ratio = (
        new_one / (1.0 - BETA_ONE**STEP) / (jnp.sqrt(new_two / (1.0 - BETA_TWO**STEP)) + ADAM_EPS)
    )
    return (weight - rate * (ratio + decay * weight), new_one, new_two)


def reduce_pair(grad_left, grad_right):
    replicas = lax.axis_size("dp")
    members = lax.axis_size("shard")
    owners = replicas * members
    left_cols = grad_left.shape[1]
    right_cols = grad_right.shape[1]
    left_rows = grad_left.shape[0] // owners
    right_rows = grad_right.shape[0] // owners
    left_owned, right_owned = (
        lax.psum_scatter(grad_left.reshape(-1), ("dp", "shard"), scatter_dimension=0, tiled=True),
        lax.psum_scatter(grad_right.reshape(-1), ("dp", "shard"), scatter_dimension=0, tiled=True),
    )
    return (left_owned.reshape(left_rows, left_cols), right_owned.reshape(right_rows, right_cols))


class Grid:
    def __init__(self, replicas):
        self.deep = replicas // 4
        index = lax.axis_index("dp")
        self.z = index // 4
        self.y = (index // 2) % 2
        self.c = index % 2
        self.x = lax.axis_index("shard")
        self.places = jnp.stack([self.z, self.y, self.c, self.x]).astype(jnp.int32)

    def pairs(self, turn):
        places = [
            (z, y, c, x)
            for z in range(self.deep)
            for y in range(2)
            for c in range(2)
            for x in range(2)
        ]
        flat = lambda z, y, c, x: ((z * 2 + y) * 2 + c) * 2 + x
        return [(flat(*p), flat(*turn(*p))) for p in places]

    def send(self, values, turn):
        return lax.ppermute(values, ("dp", "shard"), self.pairs(turn))

    def over_x(self, values):
        return self.send(values, lambda z, y, c, x: (z, y, c, 1 - x))

    def over_y(self, values):
        return self.send(values, lambda z, y, c, x: (z, 1 - y, c, x))

    def over_core(self, values):
        return self.send(values, lambda z, y, c, x: (z, y, 1 - c, x))

    def along_z(self, values, step):
        return self.send(values, lambda z, y, c, x: ((z + step) % self.deep, y, c, x))


def pick(values, index, axis):
    return lax.dynamic_index_in_dim(values, index, axis, keepdims=False)


def place_blocks(grid, own, sibling, rows, cols, *after):
    deep = grid.deep
    half = deep // 2
    spans = [(0, deep, 0, 0), (0, deep, 0, 1), (0, deep, 1, 0), (0, half, 1, 1), (half, deep, 1, 1)]

    def kernel(place_ref, *refs):
        ins = refs[:10]
        out, held, sems, sent = refs[-4:]
        z, y, c, x = [place_ref[i] for i in range(4)]
        copies = []
        for core in range(2):
            for piece, (first, last, dy, dx) in enumerate(spans):
                for step in range(first, last):
                    zz = lax.rem(z - step + deep, deep)
                    yy = lax.rem(y + dy, 2)
                    cc = lax.rem(c + core, 2)
                    xx = lax.rem(x + dx, 2)
                    block = ((zz * 2 + yy) * 2 + cc) * 2 + xx
                    turn = len(copies)
                    copies.append(
                        (
                            pltpu.make_async_copy(
                                ins[core * 5 + piece].at[step - first],
                                held.at[turn],
                                sems.at[turn],
                            ),
                            pltpu.make_async_copy(held.at[turn], out.at[block], sent.at[turn]),
                        )
                    )
        for arrive, leave in copies:
            arrive.start()
        for arrive, leave in copies:
            arrive.wait()
            leave.start()
        for arrive, leave in copies:
            leave.wait()

    blocks = deep * 8
    whole = pl.pallas_call(
        kernel,
        out_shape=jax.ShapeDtypeStruct((blocks, rows, cols), jnp.bfloat16),
        in_specs=[pl.BlockSpec(memory_space=pltpu.SMEM)]
        + [pl.BlockSpec(memory_space=pl.ANY)] * (10 + len(after)),
        out_specs=pl.BlockSpec(memory_space=pl.ANY),
        scratch_shapes=[
            pltpu.VMEM((blocks, rows, cols), jnp.bfloat16),
            pltpu.SemaphoreType.DMA((blocks,)),
            pltpu.SemaphoreType.DMA((blocks,)),
        ],
        compiler_params=pltpu.CompilerParams(vmem_limit_bytes=blocks * rows * cols * 2 + 2**21),
        cost_estimate=pl.CostEstimate(
            flops=0, bytes_accessed=blocks * rows * cols * 4, transcendentals=0
        ),
        name="place_blocks",
    )(grid.places, *own, *sibling, *after)
    return whole.reshape(blocks * rows, cols)


def hold(values, *after):
    return tuple(tie(value, *after) for value in values)


def column_of(shard, moved):
    return jnp.stack([shard] + [moved[step] for step in sorted(moved)])


def gather_two(grid, column):
    return column, grid.over_x(column), grid.over_y(column)


def gather_sends(grid, columns, *after):
    half = grid.deep // 2
    return tie(columns[1][:half], *after), tie(columns[2][half:], *after)


def gather_three(grid, sends):
    return grid.over_y(sends[0]), grid.over_x(sends[1])


def gather_end(grid, columns, last, shape, *after):
    own = (*columns, *last)
    sibling = tuple(grid.over_core(piece) for piece in own)
    return place_blocks(grid, own, sibling, *shape, *after)


def far_half(grid, values):
    cols = values.shape[1] // 2
    return lax.dynamic_slice_in_dim(values, (1 - grid.c) * cols, cols, 1)


def tie(value, *after):
    if not after:
        return value

    def kernel(*refs):
        pass

    return pl.pallas_call(
        kernel,
        out_shape=jax.ShapeDtypeStruct(value.shape, value.dtype),
        in_specs=[pl.BlockSpec(memory_space=pl.ANY)] * (1 + len(after)),
        out_specs=pl.BlockSpec(memory_space=pl.ANY),
        input_output_aliases={0: 0},
        cost_estimate=pl.CostEstimate(flops=0, bytes_accessed=0, transcendentals=0),
        name="tie",
    )(value, *after)


def sum_blocks(grid, left, right, left_far, right_far, *after):
    deep = grid.deep
    slots, width = left.shape
    cols = right_far.shape[1]
    wide = width // (deep * 2)
    rows = wide // 4
    turned = (((0,), (0,)), ((), ()))

    def kernel(place, left_ref, left_more, right_ref, right_more, *rest):
        first_sent, first_kept, second_sent, second_kept = rest[-4:]
        step = pl.program_id(0)
        total = lax.dot_general(
            left_ref[...], right_ref[...], turned, preferred_element_type=jnp.float32
        ) + lax.dot_general(
            left_more[...], right_more[...], turned, preferred_element_type=jnp.float32
        )
        parts = [total[i * rows : (i + 1) * rows, :].astype(jnp.bfloat16) for i in range(4)]
        lower = place[3] == 0

        def put(ref):
            ref[0, 0] = jnp.where(lower, parts[1], parts[0])
            ref[1, 0] = jnp.where(lower, parts[0], parts[1])

        pl.when(step < deep)(lambda: put(first_sent))
        pl.when(step >= deep)(lambda: put(first_kept))
        second_sent[0, 0] = jnp.where(lower, parts[3], parts[2])
        second_kept[0, 0] = jnp.where(lower, parts[2], parts[3])

    def block(s, place):
        return (0, (s % deep) * 2 + jnp.where(s < deep, 1 - place[1], place[1]))

    shape = jax.ShapeDtypeStruct((2, deep, rows, cols), jnp.bfloat16)
    second = pl.BlockSpec((1, 1, rows, cols), lambda s, place: (s // deep, s % deep, 0, 0))
    return pl.pallas_call(
        kernel,
        grid_spec=pltpu.PrefetchScalarGridSpec(
            num_scalar_prefetch=1,
            grid=(2 * deep,),
            in_specs=[
                pl.BlockSpec((slots, wide), block),
                pl.BlockSpec((slots, wide), block),
                pl.BlockSpec((slots, cols), lambda s, place: (0, place[2])),
                pl.BlockSpec((slots, cols), lambda s, place: (0, 0)),
            ]
            + [pl.BlockSpec(memory_space=pl.ANY)] * len(after),
            out_specs=(
                pl.BlockSpec(
                    (2, 1, rows, cols), lambda s, place: (0, jnp.minimum(s, deep - 1), 0, 0)
                ),
                pl.BlockSpec(
                    (2, 1, rows, cols), lambda s, place: (0, jnp.maximum(s - deep, 0), 0, 0)
                ),
                second,
                second,
            ),
        ),
        out_shape=(shape,) * 4,
        compiler_params=pltpu.CompilerParams(vmem_limit_bytes=28 * 2**20),
        cost_estimate=pl.CostEstimate(
            flops=4 * slots * width * cols, bytes_accessed=16 * 2**20, transcendentals=0
        ),
        name="sum_blocks",
    )(grid.places, left, left_far, right, right_far, *after)


def added(left, right):
    return (left.astype(jnp.float32) + right.astype(jnp.float32)).astype(jnp.bfloat16)


def scatter_two(grid, parts, *after):
    first_sent, first_kept, second_sent, second_kept = parts
    first_more, second_more = grid.over_y(first_sent), grid.over_x(second_sent)
    _, deep, rows, cols = first_kept.shape

    def kernel(first, first_new, second, second_new, *rest):
        first_out, first_held, second_out, second_held = rest[-4:]
        first_out[...] = added(first[0], first_new[0])
        first_held[...] = added(first[1], first_new[1])
        second_out[...] = added(second[0], second_new[0])
        second_held[...] = added(second[1], second_new[1])

    pair = pl.BlockSpec((2, 1, rows, cols), lambda z: (0, z, 0, 0))
    out = pl.BlockSpec((1, rows, cols), lambda z: (z, 0, 0))
    shape = jax.ShapeDtypeStruct((deep, rows, cols), jnp.bfloat16)
    return pl.pallas_call(
        kernel,
        grid=(deep,),
        in_specs=[pair] * 4 + [pl.BlockSpec(memory_space=pl.ANY)] * len(after),
        out_specs=(out,) * 4,
        out_shape=(shape,) * 4,
        compiler_params=pltpu.CompilerParams(vmem_limit_bytes=12 * 2**20),
        cost_estimate=pl.CostEstimate(
            flops=4 * deep * rows * cols, bytes_accessed=24 * deep * rows * cols, transcendentals=0
        ),
        name="scatter_two",
    )(first_kept, first_more, second_kept, second_more, *after)


def scatter_three(grid, parts, *after):
    first_sent, first_kept, second_sent, second_kept = parts
    first_more, second_more = grid.over_x(first_sent), grid.over_y(second_sent)
    deep, rows, cols = first_kept.shape

    def kernel(place, first, first_new, second, second_new, *rest):
        outs = rest[-deep:]
        for step in range(deep):

            @pl.when(pl.program_id(0) == step)
            def _():
                outs[step][0] = added(first[0], first_new[0])
                outs[step][1] = added(second[0], second_new[0])

    part = pl.BlockSpec((1, rows, cols), lambda k, place: (lax.rem(place[0] + k, deep), 0, 0))
    return pl.pallas_call(
        kernel,
        grid_spec=pltpu.PrefetchScalarGridSpec(
            num_scalar_prefetch=1,
            grid=(deep,),
            in_specs=[part] * 4 + [pl.BlockSpec(memory_space=pl.ANY)] * len(after),
            out_specs=(pl.BlockSpec((2, rows, cols), lambda k, place: (0, 0, 0)),) * deep,
        ),
        out_shape=(jax.ShapeDtypeStruct((2, rows, cols), jnp.bfloat16),) * deep,
        compiler_params=pltpu.CompilerParams(vmem_limit_bytes=12 * 2**20),
        cost_estimate=pl.CostEstimate(
            flops=2 * deep * rows * cols, bytes_accessed=12 * deep * rows * cols, transcendentals=0
        ),
        name="scatter_three",
    )(grid.places, first_kept, first_more, second_kept, second_more, *after)


def along(grid, chip, total, steps, *after):
    total = tie(total, *after).astype(jnp.float32)
    for step in steps:
        total = total + grid.along_z(chip[step], step).astype(jnp.float32)
    return total


def scatter_end(grid, total):
    kept = pick(total, grid.c, 0)
    arrived = grid.over_core(pick(total, 1 - grid.c, 0))
    return jnp.where(
        grid.c == 0,
        jnp.concatenate([kept, arrived], axis=1),
        jnp.concatenate([arrived, kept], axis=1),
    )


def sum_plane(grid, values):
    values = values + grid.over_core(values)
    both = grid.send(values, lambda z, y, c, x: (z, 1 - y, c, 1 - x))
    return (values + grid.over_x(values)) + (grid.over_y(values) + both)


def sum_along(grid, values):
    step = 1
    while step < grid.deep:
        values = values + grid.send(values, lambda z, y, c, x: (z ^ step, y, c, x))
        step *= 2
    return values


def rope_rows(values, cosine, sine):
    return values * cosine + pltpu.roll(values, HEAD_DIM // 2, 1) * sine


def project_heads(normed, weight, cosine, sine, gains):
    slots, width = normed.shape
    cols = weight.shape[1]
    wide = 2 * HEAD_DIM
    query_blocks, turned_blocks = HEADS // 2, (HEADS + KV_HEADS) // 2

    def kernel(normed_ref, weight_ref, cos_ref, sin_ref, gain_ref, raw_ref, low_ref):
        step = pl.program_id(0)
        block = jnp.dot(normed_ref[...], weight_ref[...], preferred_element_type=jnp.float32)

        @pl.when(step >= turned_blocks)
        def _():
            low_ref[...] = block.astype(jnp.bfloat16)

        @pl.when(step < turned_blocks)
        def _():
            raw_ref[...] = block
            gain = jnp.where(step < query_blocks, gain_ref[0:1, :], gain_ref[1:2, :])
            for head in range(2):
                part = block[:, head * HEAD_DIM : (head + 1) * HEAD_DIM]
                factor = lax.rsqrt(jnp.mean(part * part, axis=-1, keepdims=True) + EPS)
                rows = rope_rows(part * factor * gain, cos_ref[...], sin_ref[...])
                low_ref[:, head * HEAD_DIM : (head + 1) * HEAD_DIM] = rows.astype(jnp.bfloat16)

    return pl.pallas_call(
        kernel,
        grid=(cols // wide,),
        out_shape=(
            jax.ShapeDtypeStruct((slots, turned_blocks * wide), jnp.float32),
            jax.ShapeDtypeStruct((slots, cols), jnp.bfloat16),
        ),
        in_specs=[
            pl.BlockSpec((slots, width), lambda j: (0, 0)),
            pl.BlockSpec((width, wide), lambda j: (0, j)),
            pl.BlockSpec((slots, HEAD_DIM), lambda j: (0, 0)),
            pl.BlockSpec((slots, HEAD_DIM), lambda j: (0, 0)),
            pl.BlockSpec((2, HEAD_DIM), lambda j: (0, 0)),
        ],
        out_specs=(
            pl.BlockSpec((slots, wide), lambda j: (0, jnp.minimum(j, turned_blocks - 1))),
            pl.BlockSpec((slots, wide), lambda j: (0, j)),
        ),
        compiler_params=pltpu.CompilerParams(vmem_limit_bytes=14 * 2**20),
        cost_estimate=pl.CostEstimate(
            flops=8 * slots * width * cols, bytes_accessed=24 * 2**20, transcendentals=0
        ),
        name="project_heads",
    )(normed, weight, cosine, sine, gains)


def masked_weights(query, key, turn, key_turn, length):
    scores = lax.dot_general(
        query, key, (((1,), (1,)), ((), ())), preferred_element_type=jnp.float32
    ) * (HEAD_DIM ** (-0.5))
    rows = scores.shape[0]
    key_slot = lax.broadcasted_iota(jnp.int32, scores.shape, 1)
    allowed = key_slot + key_turn * rows < length
    if turn == key_turn:
        allowed &= key_slot <= lax.broadcasted_iota(jnp.int32, scores.shape, 0)
    return jnp.where(allowed, jnp.exp(scores), 0.0)


def attend(low, length, after):
    slots = low.shape[0]
    half = slots // 2
    wide = 2 * HEAD_DIM

    def kernel(len_ref, query_ref, key_ref, value_ref, *rest):
        out_ref = rest[-1]
        for head in range(2):
            cols = slice(head * HEAD_DIM, (head + 1) * HEAD_DIM)
            for turn in range(2):
                rows = slice(turn * half, (turn + 1) * half)
                keys = [slice(i * half, (i + 1) * half) for i in range(turn + 1)]
                weights = [
                    masked_weights(query_ref[rows, cols], key_ref[k, :], turn, i, len_ref[0])
                    for i, k in enumerate(keys)
                ]
                inverse = 1.0 / sum(jnp.sum(w, axis=-1, keepdims=True) for w in weights)
                context = sum(
                    jnp.dot(
                        (w * inverse).astype(jnp.bfloat16),
                        value_ref[k, :],
                        preferred_element_type=jnp.float32,
                    )
                    for w, k in zip(weights, keys)
                )
                out_ref[rows, cols] = context.astype(jnp.bfloat16)

    block = lambda offset: pl.BlockSpec((slots, HEAD_DIM), lambda g: (0, offset + g))
    pair = pl.BlockSpec((slots, wide), lambda g: (0, g))
    return pl.pallas_call(
        kernel,
        grid=(KV_HEADS,),
        out_shape=jax.ShapeDtypeStruct((slots, HEADS * HEAD_DIM), jnp.bfloat16),
        in_specs=[
            pl.BlockSpec(memory_space=pltpu.SMEM),
            pair,
            block(HEADS),
            block(HEADS + KV_HEADS),
        ]
        + [pl.BlockSpec(memory_space=pl.ANY)] * len(after),
        out_specs=pair,
        compiler_params=pltpu.CompilerParams(vmem_limit_bytes=16 * 2**20),
        cost_estimate=pl.CostEstimate(
            flops=4 * slots * slots * HEADS * HEAD_DIM,
            bytes_accessed=24 * 2**20,
            transcendentals=2 * slots * slots * HEADS,
        ),
        name="attend",
    )(length, low, low, low, *after)


def norm_back_rows(raw, gain, incoming):
    factor = lax.rsqrt(jnp.mean(raw * raw, axis=-1, keepdims=True) + EPS)
    normal = raw * factor
    scaled = incoming * gain
    inner = jnp.mean(scaled * normal, axis=-1, keepdims=True)
    return factor * (scaled - normal * inner), jnp.sum(incoming * normal, axis=0, keepdims=True)


def attend_back(low, raw, d_context, length, cosine, sine, gains, after):
    slots = low.shape[0]
    half = slots // 2
    wide = 2 * HEAD_DIM
    scale = HEAD_DIM ** (-0.5)

    def kernel(
        len_ref,
        query_ref,
        key_ref,
        value_ref,
        raw_query_ref,
        raw_key_ref,
        d_context_ref,
        cos_ref,
        sin_ref,
        gain_ref,
        *rest,
    ):
        out_ref, terms_ref = rest[-2:]
        group = pl.program_id(0)
        halves = [slice(i * half, (i + 1) * half) for i in range(2)]
        keys, values = [key_ref[k, :] for k in halves], [value_ref[k, :] for k in halves]
        d_keys, d_values = [0.0, 0.0], [0.0, 0.0]
        query_terms, key_terms = 0.0, 0.0
        flip = (((0,), (0,)), ((), ()))
        for head in range(2):
            cols = slice(head * HEAD_DIM, (head + 1) * HEAD_DIM)
            for turn in range(2):
                rows = halves[turn]
                query, d_out = query_ref[rows, cols], d_context_ref[rows, cols]
                blocks = range(turn + 1)
                weights = [masked_weights(query, keys[i], turn, i, len_ref[0]) for i in blocks]
                inverse = 1.0 / sum(jnp.sum(w, axis=-1, keepdims=True) for w in weights)
                probs = [w * inverse for w in weights]
                d_probs = [
                    lax.dot_general(
                        d_out,
                        values[i],
                        (((1,), (1,)), ((), ())),
                        preferred_element_type=jnp.float32,
                    )
                    for i in blocks
                ]
                inner = sum(jnp.sum(p * d, axis=-1, keepdims=True) for p, d in zip(probs, d_probs))
                d_query = 0.0
                for i in blocks:
                    d_scores = (probs[i] * (d_probs[i] - inner)).astype(jnp.bfloat16)
                    d_query += jnp.dot(d_scores, keys[i], preferred_element_type=jnp.float32)
                    d_keys[i] += lax.dot_general(
                        d_scores, query, flip, preferred_element_type=jnp.float32
                    )
                    d_values[i] += lax.dot_general(
                        probs[i].astype(jnp.bfloat16),
                        d_out,
                        flip,
                        preferred_element_type=jnp.float32,
                    )
                turned = rope_rows(d_query * scale, cos_ref[rows, :], -sin_ref[rows, :])
                d_raw, term = norm_back_rows(raw_query_ref[rows, cols], gain_ref[0:1, :], turned)
                place = pl.multiple_of((2 * group + head) * HEAD_DIM, HEAD_DIM)
                out_ref[rows, pl.ds(place, HEAD_DIM)] = d_raw.astype(jnp.bfloat16)
                query_terms += term
        key_cols = pl.ds(pl.multiple_of((HEADS + group) * HEAD_DIM, HEAD_DIM), HEAD_DIM)
        place = pl.multiple_of((HEADS + KV_HEADS + group) * HEAD_DIM, HEAD_DIM)
        value_cols = pl.ds(place, HEAD_DIM)
        for i, rows in enumerate(halves):
            turned = rope_rows(d_keys[i] * scale, cos_ref[rows, :], -sin_ref[rows, :])
            d_raw, term = norm_back_rows(raw_key_ref[rows, :], gain_ref[1:2, :], turned)
            out_ref[rows, key_cols] = d_raw.astype(jnp.bfloat16)
            out_ref[rows, value_cols] = d_values[i].astype(jnp.bfloat16)
            key_terms += term

        @pl.when(group == 0)
        def _():
            terms_ref[...] = jnp.zeros_like(terms_ref)

        terms_ref[0:1, :] += query_terms
        terms_ref[1:2, :] += key_terms

    block = lambda offset: pl.BlockSpec((slots, HEAD_DIM), lambda g: (0, offset + g))
    pair = pl.BlockSpec((slots, wide), lambda g: (0, g))
    table = pl.BlockSpec((slots, HEAD_DIM), lambda g: (0, 0))
    all_cols = (HEADS + 2 * KV_HEADS) * HEAD_DIM
    return pl.pallas_call(
        kernel,
        grid=(KV_HEADS,),
        out_shape=(
            jax.ShapeDtypeStruct((slots, all_cols), jnp.bfloat16),
            jax.ShapeDtypeStruct((2, HEAD_DIM), jnp.float32),
        ),
        in_specs=[
            pl.BlockSpec(memory_space=pltpu.SMEM),
            pair,
            block(HEADS),
            block(HEADS + KV_HEADS),
            pair,
            block(HEADS),
            pair,
            table,
            table,
            pl.BlockSpec((2, HEAD_DIM), lambda g: (0, 0)),
        ]
        + [pl.BlockSpec(memory_space=pl.ANY)] * len(after),
        out_specs=(
            pl.BlockSpec((slots, all_cols), lambda g: (0, 0)),
            pl.BlockSpec((2, HEAD_DIM), lambda g: (0, 0)),
        ),
        compiler_params=pltpu.CompilerParams(vmem_limit_bytes=32 * 2**20),
        cost_estimate=pl.CostEstimate(
            flops=20 * slots * slots * HEADS * HEAD_DIM,
            bytes_accessed=48 * 2**20,
            transcendentals=2 * slots * slots * HEADS,
        ),
        name="attend_back",
    )(length, low, low, low, raw, raw, d_context, cosine, sine, gains, *after)


def whole_sequence(grid, values):
    kept, sent = pick(values, grid.x, 0), pick(values, 1 - grid.x, 0)
    arrived = grid.over_x(sent)
    return jnp.where(
        grid.x == 0, jnp.concatenate([kept, arrived]), jnp.concatenate([arrived, kept])
    )


def half_sequences(grid, values, way, *after):
    halves = values.reshape(2, values.shape[0] // 2, values.shape[1])
    kept, sent = pick(halves, grid.x, 0), tie(pick(halves, 1 - grid.x, 0), *after)
    arrived = grid.over_x(sent.astype(way)).astype(values.dtype)
    return jnp.where(grid.x == 0, jnp.stack([kept, arrived]), jnp.stack([arrived, kept]))


def on_device_general(
    tokens,
    cotangent,
    lengths,
    entry_weight,
    output_weight,
    gate_weight,
    down_weight,
    entry_first,
    output_first,
    gate_first,
    down_first,
    entry_second,
    output_second,
    gate_second,
    down_second,
    gains,
    gains_first,
    gains_second,
):
    seq_count = tokens.shape[0]
    local_len = tokens.shape[1]
    group_size = HEADS // KV_HEADS
    query_cols = HEADS * HEAD_DIM
    key_cols = KV_HEADS * HEAD_DIM
    scale = HEAD_DIM ** (-0.5)
    bf16 = jnp.bfloat16
    single_float = jnp.float32
    entry_low = entry_weight.astype(bf16)
    output_low = output_weight.astype(bf16)
    gate_low = gate_weight.astype(bf16)
    down_low = down_weight.astype(bf16)
    entry_weight_whole, output_weight_whole, gate_weight_whole, down_weight_whole = (
        lax.all_gather(entry_low, ("dp", "shard"), axis=0, tiled=True),
        lax.all_gather(output_low, ("dp", "shard"), axis=0, tiled=True),
        lax.all_gather(gate_low, ("dp", "shard"), axis=0, tiled=True),
        lax.all_gather(down_low, ("dp", "shard"), axis=0, tiled=True),
    )
    g_attn = gains[:D]
    g_mlp = gains[D : 2 * D]
    g_query = gains[2 * D : 2 * D + HEAD_DIM]
    g_key = gains[2 * D + HEAD_DIM :]
    positions = lax.axis_index("shard") * local_len + jnp.arange(local_len)
    cosine, sine = angles(positions)
    cos_four = cosine[None, :, None, :]
    sin_four = sine[None, :, None, :]
    live = positions[None, :] < lengths[:, None]
    inputs = tokens.astype(single_float)
    normed_one, factor_one = norm_rows(inputs, g_attn)
    normed_reduced = normed_one.astype(bf16)
    projected = jnp.dot(normed_reduced, entry_weight_whole, preferred_element_type=single_float)
    query_raw = projected[..., :query_cols].reshape(seq_count, local_len, HEADS, HEAD_DIM)
    key_raw = projected[..., query_cols : query_cols + key_cols].reshape(
        seq_count, local_len, KV_HEADS, HEAD_DIM
    )
    value_low = projected[..., query_cols + key_cols :].astype(bf16)
    query_normed, query_factor = norm_rows(query_raw, g_query)
    key_normed, key_factor = norm_rows(key_raw, g_key)
    query_rot = rotate(query_normed, cos_four, sin_four, 1.0).astype(bf16)
    key_rot = rotate(key_normed, cos_four, sin_four, 1.0).astype(bf16)
    query_grouped = query_rot.reshape(seq_count, local_len, KV_HEADS, group_size, HEAD_DIM)
    key_all, value_all = (
        lax.all_gather(
            key_rot.reshape(seq_count, local_len, key_cols), "shard", axis=1, tiled=True
        ),
        lax.all_gather(value_low, "shard", axis=1, tiled=True),
    )
    whole_len = key_all.shape[1]
    key_heads = key_all.reshape(seq_count, whole_len, KV_HEADS, HEAD_DIM)
    value_heads = value_all.reshape(seq_count, whole_len, KV_HEADS, HEAD_DIM)
    key_place = jnp.arange(whole_len)
    allowed = (key_place[None, None, :] <= positions[None, :, None]) & (
        key_place[None, None, :] < lengths[:, None, None]
    )
    raw = (
        jnp.einsum(
            "sqgrd,skgd->sgrqk", query_grouped, key_heads, preferred_element_type=single_float
        )
        * scale
    )
    scores = jnp.where(allowed[:, None, None], raw, NEG)
    probs = jax.nn.softmax(scores, axis=-1)
    probs_low = probs.astype(bf16)
    context = jnp.einsum(
        "sgrqk,skgd->sqgrd", probs_low, value_heads, preferred_element_type=single_float
    )
    context_reduced = context.reshape(seq_count, local_len, query_cols).astype(bf16)
    attended = jnp.dot(context_reduced, output_weight_whole, preferred_element_type=single_float)
    middle = inputs + attended
    normed_two, factor_two = norm_rows(middle, g_mlp)
    second_normed_reduced = normed_two.astype(bf16)
    both = jnp.dot(second_normed_reduced, gate_weight_whole, preferred_element_type=single_float)
    gate_val = both[..., :FF]
    up_val = both[..., FF:]
    sigmoid_val = jax.nn.sigmoid(gate_val)
    silu_val = gate_val * sigmoid_val
    hidden_reduced = (silu_val * up_val).astype(bf16)
    mlp_out = jnp.dot(hidden_reduced, down_weight_whole, preferred_element_type=single_float)
    block_out = jnp.where(live[..., None], middle + mlp_out, 0.0).astype(bf16)
    backward_reduced = jnp.where(live[..., None], cotangent, jnp.zeros_like(cotangent))
    down_gradient = jnp.einsum(
        "goj,gob->jb", hidden_reduced, backward_reduced, preferred_element_type=single_float
    )
    hidden_gradient = jnp.einsum(
        "bov,gv->bog", backward_reduced, down_weight_whole, preferred_element_type=single_float
    )
    d_gate = hidden_gradient * up_val * sigmoid_val * (1.0 + gate_val * (1.0 - sigmoid_val))
    d_up = hidden_gradient * silu_val
    combined_gradient = jnp.concatenate([d_gate, d_up], axis=-1).astype(bf16)
    gate_gradient = jnp.einsum(
        "mit,mib->tb", second_normed_reduced, combined_gradient, preferred_element_type=single_float
    )
    owned_gate, owned_down = reduce_pair(gate_gradient, down_gradient)
    second_normed_gradient = jnp.einsum(
        "nar,yr->nay", combined_gradient, gate_weight_whole, preferred_element_type=single_float
    )
    d_middle_norm, mlp_gain_terms = norm_back(middle, factor_two, g_mlp, second_normed_gradient)
    d_middle = backward_reduced.astype(single_float) + d_middle_norm
    attention_gradient_reduced = d_middle.astype(bf16)
    output_gradient = jnp.einsum(
        "czm,czr->mr",
        context_reduced,
        attention_gradient_reduced,
        preferred_element_type=single_float,
    )
    context_gradient = jnp.einsum(
        "xoj,gj->xog",
        attention_gradient_reduced,
        output_weight_whole,
        preferred_element_type=single_float,
    )
    d_context_low = context_gradient.astype(bf16).reshape(
        seq_count, local_len, KV_HEADS, group_size, HEAD_DIM
    )
    d_probs = jnp.einsum(
        "sqgrd,skgd->sgrqk", d_context_low, value_heads, preferred_element_type=single_float
    )
    d_scores = probs * (d_probs - jnp.sum(probs * d_probs, axis=-1, keepdims=True))
    d_scores_low = d_scores.astype(bf16)
    d_query_rot = (
        jnp.einsum(
            "sgrqk,skgd->sqgrd", d_scores_low, key_heads, preferred_element_type=single_float
        )
        * scale
    )
    d_key_all = (
        jnp.einsum(
            "sgrqk,sqgrd->skgd", d_scores_low, query_grouped, preferred_element_type=single_float
        )
        * scale
    )
    d_value_all = jnp.einsum(
        "sgrqk,sqgrd->skgd", probs_low, d_context_low, preferred_element_type=single_float
    )
    d_key_own, d_value_own = (
        lax.psum_scatter(
            d_key_all.reshape(seq_count, whole_len, key_cols).astype(jnp.bfloat16),
            "shard",
            scatter_dimension=1,
            tiled=True,
        ).astype(jnp.float32),
        lax.psum_scatter(
            d_value_all.reshape(seq_count, whole_len, key_cols).astype(jnp.bfloat16),
            "shard",
            scatter_dimension=1,
            tiled=True,
        ).astype(jnp.float32),
    )
    d_query_turned = rotate(
        d_query_rot.reshape(seq_count, local_len, HEADS, HEAD_DIM), cos_four, sin_four, -1.0
    )
    d_key_turned = rotate(
        d_key_own.reshape(seq_count, local_len, KV_HEADS, HEAD_DIM), cos_four, sin_four, -1.0
    )
    d_query_raw, query_gain_terms = norm_back(query_raw, query_factor, g_query, d_query_turned)
    d_key_raw, key_gain_terms = norm_back(key_raw, key_factor, g_key, d_key_turned)
    projected_gradient = jnp.concatenate(
        [
            d_query_raw.reshape(seq_count, local_len, query_cols),
            d_key_raw.reshape(seq_count, local_len, key_cols),
            d_value_own,
        ],
        axis=-1,
    ).astype(bf16)
    entry_gradient = jnp.einsum(
        "mit,mib->tb", normed_reduced, projected_gradient, preferred_element_type=single_float
    )
    owned_entry, owned_output = reduce_pair(entry_gradient, output_gradient)
    first_normed_gradient = jnp.einsum(
        "nar,yr->nay", projected_gradient, entry_weight_whole, preferred_element_type=single_float
    )
    d_inputs_norm, attn_gain_terms = norm_back(inputs, factor_one, g_attn, first_normed_gradient)
    token_grad = d_middle + d_inputs_norm
    gain_terms = jnp.concatenate(
        [
            jnp.sum(attn_gain_terms, axis=(0, 1)),
            jnp.sum(mlp_gain_terms, axis=(0, 1)),
            jnp.sum(query_gain_terms, axis=(0, 1, 2)),
            jnp.sum(key_gain_terms, axis=(0, 1, 2)),
        ]
    )
    grad_gains = lax.psum(gain_terms, ("dp", "shard"))
    new_entry, new_entry_first, new_entry_second = adam(
        entry_weight, entry_first, entry_second, owned_entry, RATE_MATRIX, DECAY
    )
    new_output, new_output_first, new_output_second = adam(
        output_weight, output_first, output_second, owned_output, RATE_OUTPUT, DECAY
    )
    new_gate, new_gate_first, new_gate_second = adam(
        gate_weight, gate_first, gate_second, owned_gate, RATE_MATRIX, DECAY
    )
    new_down, new_down_first, new_down_second = adam(
        down_weight, down_first, down_second, owned_down, RATE_MATRIX, DECAY
    )
    new_gains, new_gains_first, new_gains_second = adam(
        gains, gains_first, gains_second, grad_gains, RATE_GAIN, 0.0
    )
    return (
        block_out,
        token_grad,
        new_entry,
        new_entry_first,
        new_entry_second,
        new_output,
        new_output_first,
        new_output_second,
        new_gate,
        new_gate_first,
        new_gate_second,
        new_down,
        new_down_first,
        new_down_second,
        new_gains,
        new_gains_first,
        new_gains_second,
    )


def on_device(
    tokens,
    cotangent,
    lengths,
    entry_weight,
    output_weight,
    gate_weight,
    down_weight,
    entry_first,
    output_first,
    gate_first,
    down_first,
    entry_second,
    output_second,
    gate_second,
    down_second,
    gains,
    gains_first,
    gains_second,
):
    seqs, span, width = tokens.shape
    replicas, members = lax.axis_size("dp"), lax.axis_size("shard")
    deep = replicas // 4
    rows_fit = all(
        w.shape[0] % 16 == 0 for w in (entry_weight, output_weight, gate_weight, down_weight)
    )
    if members != 2 or replicas % 8 or deep & (deep - 1) or not rows_fit:
        return on_device_general(
            tokens,
            cotangent,
            lengths,
            entry_weight,
            output_weight,
            gate_weight,
            down_weight,
            entry_first,
            output_first,
            gate_first,
            down_first,
            entry_second,
            output_second,
            gate_second,
            down_second,
            gains,
            gains_first,
            gains_second,
        )
    bf16, f32 = jnp.bfloat16, jnp.float32
    grid = Grid(replicas)
    slots = seqs * span
    query_cols = HEADS * HEAD_DIM
    entry_low, output_low, gate_low, down_low = [
        w.astype(bf16) for w in (entry_weight, output_weight, gate_weight, down_weight)
    ]
    steps = range(1, deep)
    entry_column = column_of(entry_low, {s: grid.along_z(entry_low, s) for s in steps})
    inputs_low = whole_sequence(grid, tokens)

    output_whole = lax.all_gather(output_low, ("dp", "shard"), axis=0, tiled=True)
    gate_low, down_low = hold((gate_low, down_low), entry_column)
    gate_whole = lax.all_gather(gate_low, ("dp", "shard"), axis=0, tiled=True)
    entry_columns = gather_two(grid, entry_column)
    down_column = column_of(down_low, {s: grid.along_z(down_low, s) for s in steps})

    entry_sends = gather_sends(grid, entry_columns, down_column)
    entry_last = gather_three(grid, entry_sends)

    down_column = tie(down_column, *entry_last, inputs_low)
    down_columns = gather_two(grid, down_column)
    entry_whole = gather_end(grid, entry_columns, entry_last, entry_low.shape, down_column)

    g_attn = gains[:D]
    g_mlp = gains[D : 2 * D]
    g_heads = gains[2 * D :].reshape(2, HEAD_DIM)
    cosine, sine = angles(jnp.arange(slots))
    cosine = jnp.concatenate([cosine, cosine], axis=1)
    sine = jnp.concatenate([-sine, sine], axis=1)
    length = lax.dynamic_slice_in_dim(lengths, grid.x, 1)
    live = (jnp.arange(slots) < length[0]).reshape(slots, 1)

    def dot(left, right):
        return jnp.dot(left, right, preferred_element_type=f32)

    def dot_turned(left, right):
        return lax.dot_general(left, right, (((1,), (1,)), ((), ())), preferred_element_type=f32)

    inputs = inputs_low.astype(f32)
    normed_one, factor_one = norm_rows(inputs, g_attn)
    normed_one_low = normed_one.astype(bf16)
    raw, low = project_heads(normed_one_low, entry_whole, cosine, sine, g_heads)

    context = attend(low, length, (down_column,))
    down_sends = gather_sends(grid, down_columns, context)
    down_last = gather_three(grid, down_sends)
    back = whole_sequence(grid, tie(cotangent, *down_sends))
    back = jnp.where(live, back, jnp.zeros((), bf16))
    middle = inputs + dot(context, output_whole)
    normed_two, factor_two = norm_rows(middle, g_mlp)
    normed_two_low = normed_two.astype(bf16)
    down_whole = gather_end(grid, down_columns, down_last, down_low.shape, normed_two_low)
    both = dot(normed_two_low, gate_whole)
    gate_val, up_val = both[:, :FF], both[:, FF:]
    sigmoid_val = jax.nn.sigmoid(gate_val)
    silu_val = gate_val * sigmoid_val
    hidden = (silu_val * up_val).astype(bf16)
    hidden_far = grid.over_core(hidden)
    back_far = grid.over_core(far_half(grid, back))
    d_hidden = dot_turned(back, down_whole)
    d_gate = d_hidden * up_val * sigmoid_val * (1.0 + gate_val * (1.0 - sigmoid_val))
    d_up = d_hidden * silu_val
    d_both = jnp.concatenate([d_gate, d_up], axis=-1).astype(bf16)

    d_both = tie(d_both, hidden_far, back_far)
    down_one = sum_blocks(grid, hidden, back, hidden_far, back_far)
    both_far = grid.over_core(far_half(grid, d_both))
    normed_far = grid.over_core(normed_two_low)
    gate_one = sum_blocks(grid, normed_two_low, d_both, normed_far, both_far, *down_one)
    down_two = scatter_two(grid, down_one, *gate_one)

    d_normed_two = dot_turned(tie(d_both, *down_two), gate_whole)
    d_middle_norm, mlp_gain_terms = norm_back(middle, factor_two, g_mlp, d_normed_two)
    d_middle = back.astype(f32) + d_middle_norm
    d_attended = d_middle.astype(bf16)
    context_far = grid.over_core(tie(context, d_both))
    attended_far = grid.over_core(far_half(grid, d_attended))
    d_context = dot_turned(d_attended, output_whole).astype(bf16)
    output_one = sum_blocks(
        grid, context, d_attended, context_far, attended_far, *gate_one, *down_two, d_context
    )
    gate_two = scatter_two(grid, gate_one, *output_one)
    down_chip = scatter_three(grid, down_two, *gate_two)
    normed_one_far = grid.over_core(tie(normed_one_low, d_both))

    d_projected, head_terms = attend_back(
        low,
        raw,
        d_context,
        length,
        cosine,
        sine,
        g_heads,
        (*gate_two, *down_chip, *output_one, normed_one_far),
    )
    far_steps = [s for s in steps if s == deep // 2]
    near_steps = [s for s in steps if s != deep // 2]
    output_two = scatter_two(grid, output_one, d_projected)
    gate_chip = scatter_three(grid, gate_two, *output_two)
    d_projected = tie(d_projected, *gate_chip)
    projected_far = grid.over_core(far_half(grid, d_projected))
    entry_one = sum_blocks(grid, normed_one_low, d_projected, normed_one_far, projected_far)

    down_total = along(grid, down_chip, down_chip[0], steps, *entry_one)
    owned_down = scatter_end(grid, down_total)
    gate_total = along(grid, gate_chip, gate_chip[0], near_steps, *entry_one)
    output_chip = scatter_three(grid, output_two, *entry_one)
    d_projected = tie(d_projected, *entry_one, *output_chip, gate_total)
    d_normed_one = dot_turned(d_projected, entry_whole)
    d_inputs_norm, attn_gain_terms = norm_back(inputs, factor_one, g_attn, d_normed_one)
    token_grad = d_middle + d_inputs_norm
    gain_terms = jnp.concatenate(
        [jnp.sum(attn_gain_terms, axis=0), jnp.sum(mlp_gain_terms, axis=0), head_terms.reshape(-1)]
    )
    gain_sums = sum_plane(grid, gain_terms.reshape(-1, HEAD_DIM))

    entry_two = scatter_two(grid, entry_one, gain_sums, token_grad, owned_down)
    block_out = middle + dot(tie(hidden, *entry_two), down_whole)
    block_out = jnp.where(live, block_out, 0.0).astype(bf16)
    gate_total = along(grid, gate_chip, gate_total, far_steps, block_out)
    block_out = half_sequences(grid, block_out, bf16, *entry_two)
    token_grad = half_sequences(grid, token_grad, bf16, *entry_two)
    owned_gate = scatter_end(grid, gate_total)
    output_total = along(grid, output_chip, output_chip[0], steps, *entry_two)
    owned_output = scatter_end(grid, output_total)
    grad_gains = sum_along(grid, tie(gain_sums, *entry_two)).reshape(-1)
    made_down = adam(down_weight, down_first, down_second, owned_down, RATE_MATRIX, DECAY)

    entry_chip = scatter_three(grid, entry_two, owned_output, owned_gate, made_down[0], grad_gains)
    owned_output, owned_gate = hold((owned_output, owned_gate), *entry_chip)
    made_output = adam(output_weight, output_first, output_second, owned_output, RATE_OUTPUT, DECAY)
    made_gate = adam(gate_weight, gate_first, gate_second, owned_gate, RATE_MATRIX, DECAY)
    entry_total = along(grid, entry_chip, entry_chip[0], steps, block_out, token_grad)
    owned_entry = scatter_end(grid, entry_total)
    return (
        block_out,
        token_grad,
        *adam(entry_weight, entry_first, entry_second, owned_entry, RATE_MATRIX, DECAY),
        *made_output,
        *made_gate,
        *made_down,
        *adam(gains, gains_first, gains_second, grad_gains, RATE_GAIN, 0.0),
    )


def solution(mesh):
    return jax.shard_map(
        on_device,
        mesh=mesh,
        in_specs=(
            P("dp", "shard", None),
            P("dp", "shard", None),
            P("dp"),
            P(("dp", "shard"), None),
            P(("dp", "shard"), None),
            P(("dp", "shard"), None),
            P(("dp", "shard"), None),
            P(("dp", "shard"), None),
            P(("dp", "shard"), None),
            P(("dp", "shard"), None),
            P(("dp", "shard"), None),
            P(("dp", "shard"), None),
            P(("dp", "shard"), None),
            P(("dp", "shard"), None),
            P(("dp", "shard"), None),
            P(),
            P(),
            P(),
        ),
        out_specs=(
            P("dp", "shard", None),
            P("dp", "shard", None),
            P(("dp", "shard"), None),
            P(("dp", "shard"), None),
            P(("dp", "shard"), None),
            P(("dp", "shard"), None),
            P(("dp", "shard"), None),
            P(("dp", "shard"), None),
            P(("dp", "shard"), None),
            P(("dp", "shard"), None),
            P(("dp", "shard"), None),
            P(("dp", "shard"), None),
            P(("dp", "shard"), None),
            P(("dp", "shard"), None),
            P(),
            P(),
            P(),
        ),
        check_vma=False,
    )
```
